256 devices in a mesh: rows: 8 (over z), cols: 32 (over x, y, core).
Axes of the slice: x: 4, y: 4, z: 8, core: 2. Of those that a mesh axis runs over, the one named last changes fastest.
Arguments:
- inputs: bfloat16 [64, 512, 192], P('rows', 'cols'), may hold values from -6 to 6
- step_sizes: bfloat16 [64, 512, 192], P('rows', 'cols'), may hold values from 0.5 to 2
- write_coef: bfloat16 [4, 64, 512, 16], P(None, 'rows', 'cols'), may hold values from -2 to 2
- read_coef: bfloat16 [4, 64, 512, 16], P(None, 'rows', 'cols'), may hold values from -2 to 2
- rate_table: float32 [4, 192, 16], replicated, may hold values from 0.00048828125 to 0.08
- skip_gain: float32 [192], replicated, may hold values from 0.5 to 2
- grad_out: bfloat16 [64, 512, 192], P('rows', 'cols'), may hold values from -6 to 6
Outputs:
- grad_inputs: float32 [64, 512, 192], P('rows', 'cols')
- grad_steps: float32 [64, 512, 192], P('rows', 'cols')
- grad_write: float32 [4, 64, 512, 16], P(None, 'rows', 'cols')
- grad_read: float32 [4, 64, 512, 16], P(None, 'rows', 'cols')
- grad_rates: float32 [4, 192, 16], replicated
- grad_skip: float32 [192], replicated
The draws below stay inside these ranges and needn't reach their ends.
All inputs are finite; a program needn't handle non-finite values.
Results may differ from the reference program's by a relative error of at most 0.00045.
Values sent between devices are 32-bit elements; how exact they have to be, the bound alone decides.
A program may use at most 128 MiB of HBM per device.

```python
import math
import jax
import jax.numpy as jnp
from jax import lax

DI = 192
NS = 16
SCANS = 4
H = 64
W = 512


def shard_levels(key, dims, shards, least, top_value):
    gain, own = 1.0, jax.random.fold_in(key, 6)
    for axis_at, blocks in shards:
        heights = jnp.exp(jax.random.uniform(jax.random.fold_in(own, axis_at), (blocks,), jnp.float32, least / len(shards), top_value / len(shards)))
        gain = gain * jnp.repeat(heights, dims[axis_at] // blocks).reshape([-1 if axis == axis_at else 1 for axis in range(len(dims))])
    return gain


def scatter_about(stream_key, shape, spread, most, pieces=(), dtype=jnp.bfloat16):
    loudness = shard_levels(stream_key, shape, pieces, -0.22, 0.18) if pieces else 1.0
    drawn = jax.random.normal(stream_key, shape, jnp.float32) * spread * loudness
    return jnp.minimum(jnp.maximum(drawn, -most), most).astype(dtype)


def setup_inputs(seed: int = 0) -> dict:
    splits = jax.random.split(jax.random.key(seed), 8)
    inputs = scatter_about(splits[0], (H, W, DI), 1.0, 6.0, ((0, 8), (1, 32)))
    step_sizes = jnp.clip(jnp.exp(math.log(2.0) - 1.3862944 * jax.random.uniform(splits[1], (H, W, DI), jnp.float32) ** shard_levels(splits[1], (H, W, DI), ((0, 8), (1, 32)), -0.2, 0.2)), 0.5, 2.0).astype(jnp.bfloat16)
    write_coef = scatter_about(splits[2], (SCANS, H, W, NS), 0.25, 2.0, ((1, 8), (2, 32)))
    read_coef = scatter_about(splits[3], (SCANS, H, W, NS), 0.25, 2.0, ((1, 8), (2, 32)))
    rate_table = jnp.clip(jnp.exp(jax.random.uniform(splits[4], (SCANS, DI, NS), jnp.float32, math.log(0.00048828125), math.log(0.08))), 0.00048828125, 0.08)
    skip_gain = jnp.clip(jax.random.uniform(splits[5], (DI,), jnp.float32, 0.5, 2.0), 0.5, 2.0)
    grad_out = scatter_about(splits[6], (H, W, DI), 1.0, 6.0, ((0, 8), (1, 32)))
    return dict(inputs=inputs, step_sizes=step_sizes, write_coef=write_coef, read_coef=read_coef, rate_table=rate_table, skip_gain=skip_gain, grad_out=grad_out)


def line_grads(inputs, steps, write, read, cotan, rates):
    highest = lax.Precision.HIGHEST
    decay = jnp.exp(-steps[..., None] * rates)
    scaled = steps * inputs
    drive = scaled[..., None] * write[:, :, None, :]
    start = jnp.zeros(decay.shape[1:], jnp.float32)

    def forward(state, pair):
        state = pair[0] * state + pair[1]
        return state, state

    _, states = lax.scan(forward, start, (decay, drive))
    before = jnp.concatenate([start[None], states[:-1]], axis=0)
    pulled = cotan[..., None] * read[:, :, None, :]

    def backward(message, pair):
        adjoint = pair[1] + message
        return pair[0] * adjoint, adjoint

    _, adjoint = lax.scan(backward, start, (decay, pulled), reverse=True)
    grad_rd = jnp.einsum("lmdn,lmd->lmn", states, cotan, precision=highest)
    grad_wr = jnp.einsum("lmdn,lmd->lmn", adjoint, scaled, precision=highest)
    through = jnp.einsum("lmdn,lmn->lmd", adjoint, write, precision=highest)
    memory = adjoint * decay * before
    grad_in = through * steps
    grad_st = through * inputs - jnp.einsum("lmdn,dn->lmd", memory, rates, precision=highest)
    grad_rt = -jnp.einsum("lmdn,lmd->dn", memory, steps, precision=highest)
    return grad_in, grad_st, grad_wr, grad_rd, grad_rt


def blocked(inputs, steps, write, read, cotan, rates):
    length = inputs.shape[0]
    line_count = inputs.shape[1]
    block_width = math.gcd(line_count, 16)

    def split(array):
        return array.reshape((length, line_count // block_width, block_width) + array.shape[2:]).swapaxes(0, 1)

    def joined(array):
        return array.swapaxes(0, 1).reshape((length, line_count) + array.shape[3:])

    groups = tuple(split(array) for array in (inputs, steps, write, read, cotan))
    results = lax.map(lambda group: line_grads(group[0], group[1], group[2], group[3], group[4], rates), groups)
    return joined(results[0]), joined(results[1]), joined(results[2]), joined(results[3]), jnp.sum(results[4], axis=0)


def reference(inputs, step_sizes, write_coef, read_coef, rate_table, skip_gain, grad_out):
    values = inputs.astype(jnp.float32)
    steps = step_sizes.astype(jnp.float32)
    writes = write_coef.astype(jnp.float32)
    reads = read_coef.astype(jnp.float32)
    cotan = grad_out.astype(jnp.float32)
    grad_in = skip_gain * cotan
    grad_st = jnp.zeros_like(values)
    write_list = []
    read_list = []
    rate_list = []
    for direction in range(4):
        across = direction < 2
        flipped = direction % 2 == 1

        def arrange(array):
            moved = array.transpose(1, 0, 2) if across else array
            return moved[::-1] if flipped else moved

        def restore(array):
            moved = array[::-1] if flipped else array
            return moved.transpose(1, 0, 2) if across else moved

        parts = blocked(arrange(values), arrange(steps), arrange(writes[direction]), arrange(reads[direction]), arrange(cotan), rate_table[direction])
        grad_in = grad_in + restore(parts[0])
        grad_st = grad_st + restore(parts[1])
        write_list.append(restore(parts[2]))
        read_list.append(restore(parts[3]))
        rate_list.append(parts[4])
    grad_skip = jnp.sum(cotan * values, axis=(0, 1))
    return grad_in, grad_st, jnp.stack(write_list), jnp.stack(read_list), jnp.stack(rate_list), grad_skip
```

```python
import functools
import math

import jax
import jax.numpy as jnp
from jax import lax
from jax.experimental import pallas as pl
from jax.experimental.pallas import tpu as pltpu
from jax.sharding import PartitionSpec as P

F32 = jnp.float32
T = 16
PAIRS = 8
LOG2E = 1.4426950408889634
LN2 = 0.6931471805599453
COLS = 32
ROWS = 8


def low_half():
    return lax.broadcasted_iota(jnp.int32, (8, 128), 1) < 64


def spread(coef, base, low):
    a = jnp.broadcast_to(coef[:, base : base + 1], (8, 128))
    b = jnp.broadcast_to(coef[:, base + 8 : base + 9], (8, 128))
    return a, b, jnp.where(low, a, b)


def fold(q, low):
    first = jnp.where(low, q[0], q[1])
    second = jnp.where(low, q[1], q[0])
    return first + pltpu.roll(second, 64, 1) + q[2]


def tri(f, *groups):
    return [f(*parts) for parts in zip(*groups)]


def add(a, b):
    return a + b


def mul(a, b):
    return a * b


def body(x_ref, s_ref, g_ref, w_ref, r_ref, rt_ref, sk_ref,
         gi_ref, gs_ref, gw_ref, gr_ref, fin_ref,
         flat, zmsg, rowtile, dat, coef, decays, ssend, srecv, csend, crecv, bsend, brecv,
         zrecv, keep, thr, mac, zbuf, place, th_nat, m_nat, zout, zback, asend, arecv, zsum,
         send_sem, recv_sem):
    col = lax.axis_index("cols")
    row = lax.axis_index("rows")
    low = low_half()

    barrier = pltpu.get_barrier_semaphore()

    def greet_cols(i, _):
        pl.semaphore_signal(barrier, inc=1, device_id={"cols": lax.rem(col + i, COLS)},
                            device_id_type=pl.DeviceIdType.MESH)
        return 0

    def greet_rows(i, _):
        pl.semaphore_signal(barrier, inc=1, device_id={"rows": lax.rem(row + i, ROWS)},
                            device_id_type=pl.DeviceIdType.MESH)
        return 0

    lax.fori_loop(1, COLS, greet_cols, 0)
    lax.fori_loop(1, ROWS, greet_rows, 0)

    for r in range(8):
        sv = s_ref[r].astype(F32)
        gv = g_ref[r].astype(F32)
        pv = sv * x_ref[r].astype(F32)
        at = pl.ds(r * 16, 16)
        flat[0, at, :] = sv[:, :128]
        flat[1, at, :] = pv[:, :128]
        flat[2, at, :] = gv[:, :128]
        flat[3, at, :] = jnp.concatenate([sv[:, 128:], pv[:, 128:]], axis=1)
        flat[4, at, :] = jnp.concatenate(
            [gv[:, 128:]] + [ref[k, r].astype(F32) for ref in (w_ref, r_ref) for k in (2, 3)], axis=1)
        flat[5, at, :] = jnp.concatenate(
            [gv[:, 128:]] + [ref[k, r].astype(F32) for ref in (w_ref, r_ref) for k in (0, 1)], axis=1)

    ssum = [jnp.zeros((8, 128), F32), jnp.zeros((8, 128), F32)]
    for t in range(T):
        at = pl.ds(t, 8, stride=16)
        for q in range(5):
            zmsg[q, t] = flat[q, at, :]
        rowtile[t] = flat[5, at, :]

    def unpack(t, tiles):
        s_lo, p_lo, g_lo, sp, gc = tiles
        spr = pltpu.roll(sp, 64, 1)
        gcr = pltpu.roll(gc, 64, 1)
        dat[0, t] = s_lo
        dat[1, t] = jnp.where(low, sp, spr)
        dat[2, t] = p_lo
        dat[3, t] = jnp.where(low, spr, sp)
        dat[4, t] = g_lo
        dat[5, t] = jnp.where(low, gc, gcr)
        coef[t] = gcr

    for t in range(T):
        unpack(t, (zmsg[0, t], zmsg[1, t], zmsg[2, t], zmsg[3, t], rowtile[t]))
        ssum = [ssum[0] + dat[0, t], ssum[1] + dat[1, t]]
    ssend[0] = ssum[0]
    ssend[1] = ssum[1]
    srecv[col] = ssend[...]

    pl.semaphore_wait(barrier, COLS - 1 + ROWS - 1)

    def remote(src, dst, n, **to):
        return pltpu.make_async_remote_copy(
            src_ref=src, dst_ref=dst, send_sem=send_sem.at[n], recv_sem=recv_sem.at[n],
            device_id=to, device_id_type=pl.DeviceIdType.MESH)

    def taken(ref, sem, n):
        pltpu.make_async_copy(ref, ref, sem.at[n]).wait()

    def send_z(i, _):
        to = lax.rem(row + i, ROWS)
        for c in range(2):
            remote(zmsg.at[:, 2 * to + c],
                   zrecv.at[:, pl.ds(pl.multiple_of(c * 64 + row * 8, 8), 8), :], 0, rows=to).start()
        return 0

    lax.fori_loop(1, ROWS, send_z, 0)
    for c in range(2):
        for q in range(5):
            zrecv[q, pl.ds(pl.multiple_of(c * 64 + row * 8, 8), 8), :] = zmsg[q, 2 * row + c]

    def send_s(i, _):
        to = lax.rem(col + i, COLS)
        remote(ssend, srecv.at[col], 1, cols=to).start()
        return 0

    lax.fori_loop(1, COLS, send_s, 0)

    def rates(k, p):
        return [jnp.broadcast_to(rt_ref[k, p, pl.ds(i, 1), :], (8, 128)) for i in range(3)]

    def load(q, t):
        lo = dat[2 * q, t]
        return [lo, lo, dat[2 * q + 1, t]]

    def coefs(t, p):
        return pltpu.roll(coef[t], lax.rem(128 - p, 128), 1)

    W_A, W_D, R_A, R_D = 0, 16, 32, 48
    zero3 = [jnp.zeros((8, 128), F32)] * 3

    def local_pass(p, slot, ka, kd):
        ra, rd = rates(ka, p), rates(kd, p)

        def up(t, carry):
            fa, md = carry[:3], carry[3:]
            s = load(0, t)
            da = tri(lambda a, b: jnp.exp2(a * b), s, ra)
            dd = tri(lambda a, b: jnp.exp2(a * b), s, rd)
            for i in range(3):
                decays[slot, t, i] = da[i]
                decays[slot, t, 3 + i] = dd[i]
            c = coefs(t, p)
            drive = tri(mul, load(1, t), spread(c, W_A, low))
            fa = tri(add, tri(mul, da, fa), drive)
            md = tri(mul, dd, tri(add, tri(mul, load(2, t), spread(c, R_D, low)), md))
            return (*fa, *md)

        def down(i, carry):
            t = T - 1 - i
            ma, fd = carry[:3], carry[3:]
            da = [decays[slot, t, i] for i in range(3)]
            dd = [decays[slot, t, 3 + i] for i in range(3)]
            c = coefs(t, p)
            drive = tri(mul, load(1, t), spread(c, W_D, low))
            fd = tri(add, tri(mul, dd, fd), drive)
            ma = tri(mul, da, tri(add, tri(mul, load(2, t), spread(c, R_A, low)), ma))
            return (*ma, *fd)

        a = lax.fori_loop(0, T, up, (*zero3, *zero3), unroll=True)
        b = lax.fori_loop(0, T, down, (*zero3, *zero3), unroll=True)
        return a[:3], b[:3], b[3:], a[3:]

    def final_pass(p, slot, ka, kd, starts):
        ra, rd = rates(ka, p), rates(kd, p)
        fa0, ma0, fd0, md0 = starts

        def up(t, carry):
            h, m = carry[:3], carry[3:]
            da = [decays[slot, t, i] for i in range(3)]
            dd = [decays[slot, t, 3 + i] for i in range(3)]
            sx, g = load(1, t), load(2, t)
            c = coefs(t, p)
            db = tri(mul, da, h)
            h = tri(add, db, tri(mul, sx, spread(c, W_A, low)))
            adj = tri(add, tri(mul, g, spread(c, R_D, low)), m)
            for i in range(3):
                keep[t, i] = db[i]
                keep[t, 3 + i] = adj[i]
            zbuf[2, p, t] = fold(tri(mul, h, g), low)
            zbuf[1, p, t] = fold(tri(mul, adj, sx), low)
            th = tri(mul, adj, spread(c, W_D, low))
            thr[0, t] += th[0] + th[1]
            thr[1, t] += th[2]
            return (*h, *tri(mul, dd, adj))

        def down(i, carry):
            t = T - 1 - i
            m, h, acc_a, acc_d = carry[:3], carry[3:6], carry[6:9], carry[9:]
            da = [decays[slot, t, i] for i in range(3)]
            dd = [decays[slot, t, 3 + i] for i in range(3)]
            s, sx, g = load(0, t), load(1, t), load(2, t)
            c = coefs(t, p)
            db = tri(mul, dd, h)
            h = tri(add, db, tri(mul, sx, spread(c, W_D, low)))
            adj = tri(add, tri(mul, g, spread(c, R_A, low)), m)
            zbuf[3, p, t] = fold(tri(mul, h, g), low)
            zbuf[0, p, t] = fold(tri(mul, adj, sx), low)
            th = tri(mul, adj, spread(c, W_A, low))
            thr[0, t] += th[0] + th[1]
            thr[1, t] += th[2]
            mem_a = tri(mul, adj, [keep[t, i] for i in range(3)])
            mem_d = tri(mul, [keep[t, 3 + i] for i in range(3)], db)
            mr = tri(add, tri(mul, mem_a, ra), tri(mul, mem_d, rd))
            mac[0, t] += mr[0] + mr[1]
            mac[1, t] += mr[2]
            acc_a = tri(add, acc_a, tri(mul, mem_a, s))
            acc_d = tri(add, acc_d, tri(mul, mem_d, s))
            return (*tri(mul, da, adj), *h, *acc_a, *acc_d)

        lax.fori_loop(0, T, up, (*fa0, *md0), unroll=True)
        out = lax.fori_loop(0, T, down, (*ma0, *fd0, *zero3, *zero3), unroll=True)
        for k, acc in ((ka, out[6:9]), (kd, out[9:])):
            for i in range(3):
                asend[k * PAIRS + p, pl.ds(i, 1), :] = -jnp.sum(acc[i], axis=0, keepdims=True)

    def clear():
        thr[...] = jnp.zeros_like(thr)
        mac[...] = jnp.zeros_like(mac)

    def channel_sums():
        total = None
        for q in range(4):
            whole = jnp.concatenate([zbuf[q, p].reshape(128, 128) for p in range(PAIRS)], axis=1)
            high = whole.astype(jnp.bfloat16)
            rest = (whole - high.astype(F32)).astype(jnp.bfloat16)
            part = jnp.dot(high, place[...], preferred_element_type=F32)
            part = part + jnp.dot(rest, place[...], preferred_element_type=F32)
            part = part if q == 0 else pltpu.roll(part, 16 * q, 1)
            total = part if total is None else total + part
        return total.reshape(T, 8, 128)

    def both_halves(v):
        return v + pltpu.roll(v, 64, 1)

    def row_local(p, _):
        fa, ma, fd, md = local_pass(p, p, 0, 1)
        for q, parts in enumerate((fa, ma, fd, md)):
            for i in range(3):
                csend[q * PAIRS + p, i] = parts[i]
        return 0

    lax.fori_loop(0, PAIRS, row_local, 0)

    def send_c(i, _):
        to = lax.rem(col + i, COLS)
        remote(csend.at[to], crecv.at[col], 2, cols=to).start()
        return 0

    lax.fori_loop(1, COLS, send_c, 0)
    crecv[col] = csend[col]

    spot_k = lax.broadcasted_iota(jnp.int32, (128, 128), 0) // 64 * 8
    spot_n = lax.broadcasted_iota(jnp.int32, (128, 128), 1)
    for p in range(PAIRS):
        place[pl.ds(p * 128, 128), :] = jnp.where(spot_n == spot_k + p, 1.0, 0.0).astype(jnp.bfloat16)
    skip = [jnp.zeros((1, 192), F32)]
    for r in range(8):
        skip[0] = skip[0] + jnp.sum(g_ref[r].astype(F32) * x_ref[r].astype(F32), axis=0, keepdims=True)
    skip_lo = skip[0][:, :128]
    skip_hi = jnp.concatenate([skip[0][:, 128:], skip[0][:, 128:]], axis=1)
    skip_tile = jnp.concatenate([jnp.zeros((3, 128), F32), skip_lo, skip_hi, jnp.zeros((3, 128), F32)], axis=0)

    def put_skip(o, _):
        asend[o] = skip_tile
        return 0

    lax.fori_loop(0, COLS, put_skip, 0)
    clear()

    taken(srecv.at[pl.ds(0, COLS - 1)], recv_sem, 1)
    taken(crecv.at[pl.ds(0, COLS - 1)], recv_sem, 2)
    kind = col // PAIRS
    pair = lax.rem(col, PAIRS)
    falls = jnp.where((kind == 1) | (kind == 2), 1, 0)
    own_rates = rates(kind // 2, pair)

    def chain(i, carry):
        b = i + falls * (COLS - 1 - 2 * i)
        for j in range(3):
            bsend[b, j] = carry[j]
        s_lo, s_hi = srecv[b, 0], srecv[b, 1]
        held = tri(lambda a, r: jnp.exp2(a * r), [s_lo, s_lo, s_hi], own_rates)
        return tuple(held[j] * carry[j] + crecv[b, j] for j in range(3))

    lax.fori_loop(0, COLS, chain, tuple(zero3), unroll=True)

    def send_b(i, _):
        to = lax.rem(col + i, COLS)
        remote(bsend.at[to], brecv.at[col], 3, cols=to).start()
        return 0

    lax.fori_loop(1, COLS, send_b, 0)
    brecv[col] = bsend[col]

    taken(brecv.at[pl.ds(0, COLS - 1)], recv_sem, 3)

    def row_final(p, _):
        starts = [[brecv[q * PAIRS + p, i] for i in range(3)] for q in range(4)]
        final_pass(p, p, 0, 1, starts)
        return 0

    lax.fori_loop(0, PAIRS, row_final, 0)
    sums = channel_sums()
    for t in range(T):
        at = pl.ds(t, 8, stride=16)
        th_nat[0, at, :] = thr[0, t]
        th_nat[1, at, :] = both_halves(thr[1, t])
        m_nat[0, at, :] = mac[0, t]
        m_nat[1, at, :] = both_halves(mac[1, t])
        flat[5, at, :] = sums[t]

    taken(zrecv.at[:, pl.ds(0, 112), :], recv_sem, 0)
    for t in range(T):
        at = pl.ds(t, 8, stride=16)
        unpack(t, [zrecv[q, at, :] for q in range(5)])
    zs = [jnp.zeros((8, 128), F32), jnp.zeros((8, 128), F32)]
    for t in range(T):
        zs = [zs[0] + dat[0, t], zs[1] + dat[1, t]]
    clear()
    chunk = lax.rem(lax.broadcasted_iota(jnp.int32, (8, 128), 0), 4)

    def line_final(p, carry):
        zs_lo, zs_hi = carry
        fa, ma, fd, md = local_pass(p, 0, 2, 3)
        ha = tri(lambda a, r: jnp.exp2(a * r), [zs_lo, zs_lo, zs_hi], rates(2, p))
        hd = tri(lambda a, r: jnp.exp2(a * r), [zs_lo, zs_lo, zs_hi], rates(3, p))

        def across(held, ends, rising):
            out = []
            for a, f in zip(held, ends):
                st = jnp.zeros((8, 128), F32)
                for _ in range(3):
                    moved = pltpu.roll(a * st + f, 1 if rising else 7, 0)
                    st = jnp.where(chunk > 0 if rising else chunk < 3, moved, 0.0)
                out.append(st)
            return out

        final_pass(p, 0, 2, 3, [across(ha, fa, True), across(ha, ma, False),
                                across(hd, fd, False), across(hd, md, True)])
        return carry

    lax.fori_loop(0, PAIRS, line_final, tuple(zs))
    sums = channel_sums()
    for t in range(T):
        at = pl.ds(t, 8, stride=16)
        zout[0, at, :] = thr[0, t]
        zout[1, at, :] = mac[0, t]
        zout[2, at, :] = jnp.where(low, both_halves(thr[1, t]), both_halves(mac[1, t]))
        zout[3, at, :] = sums[t]

    def send_back(i, _):
        to = lax.rem(row + i, ROWS)
        for c in range(2):
            remote(zout.at[:, pl.ds(pl.multiple_of(c * 64 + to * 8, 8), 8), :],
                   zback.at[:, pl.ds(pl.multiple_of(row * 16 + c * 8, 8), 8), :], 4, rows=to).start()
        return 0

    lax.fori_loop(1, ROWS, send_back, 0)
    for c in range(2):
        zback[:, pl.ds(pl.multiple_of(row * 16 + c * 8, 8), 8), :] = (
            zout[:, pl.ds(pl.multiple_of(c * 64 + row * 8, 8), 8), :])

    def send_a(i, _):
        to = lax.rem(col + i, COLS)
        remote(asend.at[to], arecv.at[col], 5, cols=to).start()
        return 0

    lax.fori_loop(1, COLS, send_a, 0)
    arecv[col] = asend[col]
    taken(arecv.at[pl.ds(0, COLS - 1)], recv_sem, 5)
    total = arecv[0]
    for b in range(1, COLS):
        total = total + arecv[b]
    zsum[row] = total

    def send_zsum(i, _):
        to = lax.rem(row + i, ROWS)
        remote(zsum.at[row], zsum.at[row], 6, rows=to).start()
        return 0

    lax.fori_loop(1, ROWS, send_zsum, 0)

    taken(zback.at[:, pl.ds(0, 112), :], recv_sem, 4)
    for r in range(8):
        back = pl.ds(r, 16, stride=8)
        at = pl.ds(r * 16, 16)
        packed = zback[2, back, :]
        th_lo = th_nat[0, at, :] + zback[0, back, :]
        m_lo = m_nat[0, at, :] + zback[1, back, :]
        th_hi = (th_nat[1, at, :] + packed)[:, :64]
        m_hi = (m_nat[1, at, :] + pltpu.roll(packed, 64, 1))[:, :64]
        xv = x_ref[r].astype(F32)
        sv = s_ref[r].astype(F32)
        gv = g_ref[r].astype(F32)
        gi_ref[r, :, :128] = sk_ref[:, :128] * gv[:, :128] + sv[:, :128] * th_lo
        gi_ref[r, :, 128:] = sk_ref[:, 128:] * gv[:, 128:] + sv[:, 128:] * th_hi
        gs_ref[r, :, :128] = th_lo * xv[:, :128] + LN2 * m_lo
        gs_ref[r, :, 128:] = th_hi * xv[:, 128:] + LN2 * m_hi
        mine = flat[5, at, :]
        other = zback[3, back, :]
        gw_ref[0, r] = mine[:, :16]
        gw_ref[1, r] = mine[:, 16:32]
        gr_ref[0, r] = mine[:, 32:48]
        gr_ref[1, r] = mine[:, 48:64]
        gw_ref[2, r] = other[:, :16]
        gw_ref[3, r] = other[:, 16:32]
        gr_ref[2, r] = other[:, 32:48]
        gr_ref[3, r] = other[:, 48:64]

    pltpu.make_async_copy(zsum.at[pl.ds(0, ROWS - 1)], zsum.at[pl.ds(0, ROWS - 1)], recv_sem.at[6]).wait()
    total = zsum[0]
    for b in range(1, ROWS):
        total = total + zsum[b]
    fin_ref[col] = total

    def send_fin(i, _):
        to = lax.rem(col + i, COLS)
        remote(fin_ref.at[col], fin_ref.at[col], 7, cols=to).start()
        return 0

    lax.fori_loop(1, COLS, send_fin, 0)
    taken(fin_ref.at[pl.ds(0, COLS - 1)], recv_sem, 7)

    taken(zrecv.at[:, pl.ds(0, 112), :], send_sem, 0)
    taken(srecv.at[pl.ds(0, COLS - 1)], send_sem, 1)
    taken(crecv.at[pl.ds(0, COLS - 1)], send_sem, 2)
    taken(brecv.at[pl.ds(0, COLS - 1)], send_sem, 3)
    taken(zback.at[:, pl.ds(0, 112), :], send_sem, 4)
    taken(arecv.at[pl.ds(0, COLS - 1)], send_sem, 5)
    taken(zsum.at[pl.ds(0, ROWS - 1)], send_sem, 6)
    taken(fin_ref.at[pl.ds(0, COLS - 1)], send_sem, 7)


def on_device(inputs, step_sizes, write_coef, read_coef, rate_table, skip_gain, grad_out):
    by_state = (rate_table * (-LOG2E)).transpose(0, 2, 1)
    lo = by_state[:, :, :128].reshape(4, 2, 8, 128)
    hi = by_state[:, :, 128:].reshape(4, 2, 8, 64)
    table = jnp.stack([lo[:, 0], lo[:, 1], jnp.concatenate([hi[:, 0], hi[:, 1]], axis=-1)], axis=2)
    vm = pl.BlockSpec(memory_space=pltpu.VMEM)
    shapes = [
        (6, 128, 128),
        (5, T, 8, 128),
        (T, 8, 128),
        (6, T, 8, 128),
        (T, 8, 128),
        (PAIRS, T, 6, 8, 128),
        (2, 8, 128),
        (COLS, 2, 8, 128),
        (COLS, 3, 8, 128),
        (COLS, 3, 8, 128),
        (COLS, 3, 8, 128),
        (COLS, 3, 8, 128),
        (5, 128, 128),
        (T, 6, 8, 128),
        (2, T, 8, 128),
        (2, T, 8, 128),
        (4, PAIRS, T, 8, 128),
        None,
        (2, 128, 128),
        (2, 128, 128),
        (4, 128, 128),
        (4, 128, 128),
        (COLS, 8, 128),
        (COLS, 8, 128),
        (ROWS, 8, 128),
    ]
    scratch = [pltpu.VMEM((PAIRS * 128, 128), jnp.bfloat16) if s is None else pltpu.VMEM(s, F32) for s in shapes]
    scratch += [pltpu.SemaphoreType.DMA((8,)), pltpu.SemaphoreType.DMA((8,))]
    gi, gs, gw, gr, fin = pl.pallas_call(
        body,
        out_shape=[
            jax.ShapeDtypeStruct((8, 16, 192), F32),
            jax.ShapeDtypeStruct((8, 16, 192), F32),
            jax.ShapeDtypeStruct((4, 8, 16, 16), F32),
            jax.ShapeDtypeStruct((4, 8, 16, 16), F32),
            jax.ShapeDtypeStruct((COLS, 8, 128), F32),
        ],
        in_specs=[vm] * 7,
        out_specs=[vm] * 5,
        scratch_shapes=scratch,
        compiler_params=pltpu.CompilerParams(
            collective_id=0, has_side_effects=True, vmem_limit_bytes=32 * 1024 * 1024),
    )(inputs, step_sizes, grad_out, write_coef, read_coef, table, skip_gain.reshape(1, 192))
    parts = fin.reshape(4, 8, 8, 128)
    lo = parts[:, :, :2].transpose(0, 3, 2, 1).reshape(4, 128, 16)
    hi = parts[:, :, 2].reshape(4, 8, 2, 64).transpose(0, 3, 2, 1).reshape(4, 64, 16)
    grad_rates = jnp.concatenate([lo, hi], axis=1)
    grad_skip = jnp.concatenate([fin[0, 3], fin[0, 4, :64]])
    return gi, gs, gw, gr, grad_rates, grad_skip


def solution(mesh):
    cells, coefs = P("rows", "cols", None), P(None, "rows", "cols", None)
    return jax.shard_map(
        on_device, mesh=mesh, in_specs=(cells, cells, coefs, coefs, P(), P(), cells),
        out_specs=(cells, cells, coefs, coefs, P(), P()), check_vma=False)
```

```python
import functools
import math

import jax
import jax.numpy as jnp
from jax import lax
from jax.experimental import pallas as pl
from jax.experimental.pallas import tpu as pltpu
from jax.sharding import PartitionSpec as P

F32 = jnp.float32
T = 16
PAIRS = 8
LOG2E = 1.4426950408889634
LN2 = 0.6931471805599453
COLS = 32
ROWS = 8


def low_half():
    return lax.broadcasted_iota(jnp.int32, (8, 128), 1) < 64


def fold(q, low):
    return jnp.where(low, q[0], q[1]) + q[2], jnp.where(low, q[1], q[0])


def tri(f, *groups):
    return [f(*parts) for parts in zip(*groups)]


def add(a, b):
    return a + b


def mul(a, b):
    return a * b


def body(x_ref, s_ref, g_ref, w_ref, r_ref, rt_ref, sk_ref,
         gi_ref, gs_ref, gc_ref, fin_ref,
         flat, zmsg, rowtile, dat_r, dat_z, decays, ssend, srecv, csend, crecv, bsend, brecv,
         zrecv, ztile, keep, acc_r, acc_z, zbuf, pick, place, spread_r, spread_z, shift, nat,
         zout, zback, asend, arecv, zsum, send_sem, recv_sem):
    col = lax.axis_index("cols")
    row = lax.axis_index("rows")
    low = low_half()

    barrier = pltpu.get_barrier_semaphore()

    def greet_cols(i, _):
        pl.semaphore_signal(barrier, inc=1, device_id={"cols": lax.rem(col + i, COLS)},
                            device_id_type=pl.DeviceIdType.MESH)
        return 0

    def greet_rows(i, _):
        pl.semaphore_signal(barrier, inc=1, device_id={"rows": lax.rem(row + i, ROWS)},
                            device_id_type=pl.DeviceIdType.MESH)
        return 0

    lax.fori_loop(1, COLS, greet_cols, 0)
    lax.fori_loop(1, ROWS, greet_rows, 0)

    def remote(src, dst, n, **to):
        return pltpu.make_async_remote_copy(
            src_ref=src, dst_ref=dst, send_sem=send_sem.at[n], recv_sem=recv_sem.at[n],
            device_id=to, device_id_type=pl.DeviceIdType.MESH)

    def taken(ref, sem, n):
        pltpu.make_async_copy(ref, ref, sem.at[n]).wait()

    for r in range(8):
        sv = s_ref[r].astype(F32)
        gv = g_ref[r].astype(F32)
        pv = sv * x_ref[r].astype(F32)
        at = pl.ds(r * 16, 16)
        flat[0, at, :] = sv[:, :128]
        flat[1, at, :] = pv[:, :128]
        flat[2, at, :] = gv[:, :128]
        flat[3, at, :] = jnp.concatenate([sv[:, 128:], pv[:, 128:]], axis=1)
        flat[4, at, :] = jnp.concatenate(
            [gv[:, 128:]] + [ref[k, r].astype(F32) for ref in (w_ref, r_ref) for k in (2, 3)], axis=1)
        flat[5, at, :] = jnp.concatenate(
            [gv[:, 128:]] + [ref[k, r].astype(F32) for ref in (w_ref, r_ref) for k in (0, 1)], axis=1)

    for t in range(T):
        at = pl.ds(t, 8, stride=16)
        for q in range(5):
            zmsg[q, t] = flat[q, at, :]
        rowtile[t] = flat[5, at, :]

    def unpack(dat, t, tiles):
        s_lo, p_lo, g_lo, sp, gc = tiles
        spr = pltpu.roll(sp, 64, 1)
        dat[0, t] = s_lo
        dat[1, t] = jnp.where(low, sp, spr)
        dat[2, t] = p_lo
        dat[3, t] = jnp.where(low, spr, sp)
        dat[4, t] = g_lo
        dat[5, t] = jnp.where(low, gc, pltpu.roll(gc, 64, 1))

    def step_sums(dat):
        lo, hi = dat[0, 0], dat[1, 0]
        for t in range(1, T):
            lo, hi = lo + dat[0, t], hi + dat[1, t]
        return lo, hi

    for t in range(T):
        unpack(dat_r, t, (zmsg[0, t], zmsg[1, t], zmsg[2, t], zmsg[3, t], rowtile[t]))
    ssum = step_sums(dat_r)
    ssend[0] = ssum[0]
    ssend[1] = ssum[1]
    srecv[col] = ssend[...]

    pick_j = lax.broadcasted_iota(jnp.int32, (128, 128), 0)
    pick_up = pick_j - jnp.where(lax.broadcasted_iota(jnp.int32, (128, 128), 1) < 64, 0, 8)

    def fill_pick(p, _):
        for which in range(4):
            base = 64 + 16 * which
            for i, (source, start) in enumerate(((pick_j, base), (pick_j, base + 8), (pick_up, base))):
                pick[p, :, pl.ds((which * 3 + i) * 128, 128)] = jnp.where(
                    source == start + p, 1.0, 0.0).astype(jnp.bfloat16)
        return 0

    lax.fori_loop(0, PAIRS, fill_pick, 0)

    pl.semaphore_wait(barrier, COLS - 1 + ROWS - 1)

    def send_z(i, _):
        to = lax.rem(row + i, ROWS)
        for c in range(2):
            remote(zmsg.at[:, 2 * to + c],
                   zrecv.at[:, pl.ds(pl.multiple_of(c * 64 + row * 8, 8), 8), :], 0, rows=to).start()
        return 0

    lax.fori_loop(1, ROWS, send_z, 0)
    for c in range(2):
        for q in range(5):
            zrecv[q, pl.ds(pl.multiple_of(c * 64 + row * 8, 8), 8), :] = zmsg[q, 2 * row + c]

    def send_s(i, _):
        to = lax.rem(col + i, COLS)
        remote(ssend, srecv.at[col], 1, cols=to).start()
        return 0

    lax.fori_loop(1, COLS, send_s, 0)

    def rates(k, p):
        return [jnp.broadcast_to(rt_ref[k, p, pl.ds(i, 1), :], (8, 128)) for i in range(3)]

    def load(dat, q, t):
        lo = dat[2 * q, t]
        return [lo, lo, dat[2 * q + 1, t]]

    W_A, W_D, R_A, R_D = 0, 1, 2, 3
    zero3 = [jnp.zeros((8, 128), F32)] * 3

    def coefs(wide, slot, t, which):
        return [wide[slot, pl.ds(t * 8, 8), pl.ds((which * 3 + i) * 128, 128)] for i in range(3)]

    def held(t, slot):
        return [decays[slot, t, i] for i in range(3)], [decays[slot, t, 3 + i] for i in range(3)]

    def local_pass(p, slot, dslot, ka, kd, dat, wide, tile):
        wide[slot] = jnp.dot(tile[...], pick[p], preferred_element_type=F32)
        ra, rd = rates(ka, p), rates(kd, p)

        def up(t, carry):
            fa, md = carry[:3], carry[3:]
            s = load(dat, 0, t)
            da = tri(lambda a, b: jnp.exp2(a * b), s, ra)
            dd = tri(lambda a, b: jnp.exp2(a * b), s, rd)
            for i in range(3):
                decays[dslot, t, i] = da[i]
                decays[dslot, t, 3 + i] = dd[i]
            drive = tri(mul, load(dat, 1, t), coefs(wide, slot, t, W_A))
            fa = tri(add, tri(mul, da, fa), drive)
            md = tri(mul, dd, tri(add, tri(mul, load(dat, 2, t), coefs(wide, slot, t, R_D)), md))
            return (*fa, *md)

        def down(i, carry):
            t = T - 1 - i
            ma, fd = carry[:3], carry[3:]
            da, dd = held(t, dslot)
            drive = tri(mul, load(dat, 1, t), coefs(wide, slot, t, W_D))
            fd = tri(add, tri(mul, dd, fd), drive)
            ma = tri(mul, da, tri(add, tri(mul, load(dat, 2, t), coefs(wide, slot, t, R_A)), ma))
            return (*ma, *fd)

        a = lax.fori_loop(0, T, up, (*zero3, *zero3), unroll=True)
        b = lax.fori_loop(0, T, down, (*zero3, *zero3), unroll=True)
        return a[:3], b[:3], b[3:], a[3:]

    def final_pass(p, slot, dslot, ka, kd, dat, wide, acc, starts):
        ra, rd = rates(ka, p), rates(kd, p)
        fa0, ma0, fd0, md0 = starts

        def put(q, t, parts):
            zbuf[q, p, 0, t], zbuf[q, p, 1, t] = fold(parts, low)

        def up(t, carry):
            h, m = carry[:3], carry[3:]
            da, dd = held(t, dslot)
            sx, g = load(dat, 1, t), load(dat, 2, t)
            db = tri(mul, da, h)
            h = tri(add, db, tri(mul, sx, coefs(wide, slot, t, W_A)))
            adj = tri(add, tri(mul, g, coefs(wide, slot, t, R_D)), m)
            for i in range(3):
                keep[t, i] = db[i]
                keep[t, 3 + i] = adj[i]
            put(2, t, tri(mul, h, g))
            put(1, t, tri(mul, adj, sx))
            th = tri(mul, adj, coefs(wide, slot, t, W_D))
            keep[t, 6] = th[0] + th[1]
            keep[t, 7] = th[2]
            return (*h, *tri(mul, dd, adj))

        def down(i, carry):
            t = T - 1 - i
            m, h, acc_a, acc_d = carry[:3], carry[3:6], carry[6:9], carry[9:]
            da, dd = held(t, dslot)
            s, sx, g = load(dat, 0, t), load(dat, 1, t), load(dat, 2, t)
            db = tri(mul, dd, h)
            h = tri(add, db, tri(mul, sx, coefs(wide, slot, t, W_D)))
            adj = tri(add, tri(mul, g, coefs(wide, slot, t, R_A)), m)
            put(3, t, tri(mul, h, g))
            put(0, t, tri(mul, adj, sx))
            th = tri(mul, adj, coefs(wide, slot, t, W_A))
            acc[0, t] += keep[t, 6] + (th[0] + th[1])
            acc[1, t] += keep[t, 7] + th[2]
            mem_a = tri(mul, adj, [keep[t, i] for i in range(3)])
            mem_d = tri(mul, [keep[t, 3 + i] for i in range(3)], db)
            mr = tri(add, tri(mul, mem_a, ra), tri(mul, mem_d, rd))
            acc[2, t] += mr[0] + mr[1]
            acc[3, t] += mr[2]
            acc_a = tri(add, acc_a, tri(mul, mem_a, s))
            acc_d = tri(add, acc_d, tri(mul, mem_d, s))
            return (*tri(mul, da, adj), *h, *acc_a, *acc_d)

        lax.fori_loop(0, T, up, (*fa0, *md0), unroll=True)
        out = lax.fori_loop(0, T, down, (*ma0, *fd0, *zero3, *zero3), unroll=True)
        for k, sums in ((ka, out[6:9]), (kd, out[9:])):
            for i in range(3):
                asend[k * PAIRS + p, pl.ds(i, 1), :] = -jnp.sum(sums[i], axis=0, keepdims=True)

    def channel_sums():
        total = None
        for q in range(4):
            whole = jnp.concatenate(
                [zbuf[q, p, j].reshape(128, 128) for p in range(PAIRS) for j in range(2)], axis=1)
            high = whole.astype(jnp.bfloat16)
            rest = (whole - high.astype(F32)).astype(jnp.bfloat16)
            part = jnp.dot(high, place[q], preferred_element_type=F32)
            part = part + jnp.dot(rest, place[q], preferred_element_type=F32)
            total = part if total is None else total + part
        return total.reshape(T, 8, 128)

    def settle(acc, t):
        th, m = acc[1, t], acc[3, t]
        return jnp.where(low, th, m) + pltpu.roll(jnp.where(low, m, th), 64, 1)

    tile_r = rowtile[...].reshape(128, 128).astype(jnp.bfloat16)
    ztile[...] = tile_r

    def row_local(p, _):
        fa, ma, fd, md = local_pass(p, p, p, 0, 1, dat_r, spread_r, ztile)
        for q, parts in enumerate((fa, ma, fd, md)):
            for i in range(3):
                csend[q * PAIRS + p, i] = parts[i]
        return 0

    lax.fori_loop(0, PAIRS, row_local, 0)

    def send_c(i, _):
        to = lax.rem(col + i, COLS)
        remote(csend.at[to], crecv.at[col], 2, cols=to).start()
        return 0

    lax.fori_loop(1, COLS, send_c, 0)
    crecv[col] = csend[col]

    place_k = lax.broadcasted_iota(jnp.int32, (128, 128), 0) // 64 * 8
    place_n = lax.broadcasted_iota(jnp.int32, (128, 128), 1)

    def fill_place(p, _):
        for q in range(4):
            for j, source in enumerate((place_n - place_k, place_n + place_k - 8)):
                place[q, pl.ds(pl.multiple_of(p * 256 + j * 128, 128), 128), :] = jnp.where(
                    source == 16 * q + p, 1.0, 0.0).astype(jnp.bfloat16)
        return 0

    lax.fori_loop(0, PAIRS, fill_place, 0)
    skip = jnp.zeros((1, 192), F32)
    for r in range(8):
        skip = skip + jnp.sum(g_ref[r].astype(F32) * x_ref[r].astype(F32), axis=0, keepdims=True)
    skip_lo = skip[:, :128]
    skip_hi = jnp.concatenate([skip[:, 128:], skip[:, 128:]], axis=1)
    skip_tile = jnp.concatenate([jnp.zeros((3, 128), F32), skip_lo, skip_hi, jnp.zeros((3, 128), F32)], axis=0)

    def put_skip(o, _):
        asend[o] = skip_tile
        return 0

    lax.fori_loop(0, COLS, put_skip, 0)
    acc_r[...] = jnp.zeros_like(acc_r)
    acc_z[...] = jnp.zeros_like(acc_z)
    shift[...] = jnp.zeros_like(shift)

    taken(srecv.at[pl.ds(0, COLS - 1)], recv_sem, 1)
    taken(crecv.at[pl.ds(0, COLS - 1)], recv_sem, 2)
    kind = col // PAIRS
    pair = lax.rem(col, PAIRS)
    falls = jnp.where((kind == 1) | (kind == 2), 1, 0)
    own_rates = rates(kind // 2, pair)

    def chain(i, carry):
        b = i + falls * (COLS - 1 - 2 * i)
        for j in range(3):
            bsend[b, j] = carry[j]
        s_lo, s_hi = srecv[b, 0], srecv[b, 1]
        kept = tri(lambda a, r: jnp.exp2(a * r), [s_lo, s_lo, s_hi], own_rates)
        return tuple(kept[j] * carry[j] + crecv[b, j] for j in range(3))

    lax.fori_loop(0, COLS, chain, tuple(zero3), unroll=True)

    def send_b(i, _):
        to = lax.rem(col + i, COLS)
        remote(bsend.at[to], brecv.at[col], 3, cols=to).start()
        return 0

    lax.fori_loop(1, COLS, send_b, 0)
    brecv[col] = bsend[col]

    taken(zrecv.at[:, pl.ds(0, 112), :], recv_sem, 0)
    for t in range(T):
        at = pl.ds(t, 8, stride=16)
        tiles = [zrecv[q, at, :] for q in range(5)]
        unpack(dat_z, t, tiles)
        rowtile[t] = tiles[4]
    ztile[...] = rowtile[...].reshape(128, 128).astype(jnp.bfloat16)
    chunk = lax.rem(lax.broadcasted_iota(jnp.int32, (8, 128), 0), 4)
    from_chunk = {1: [chunk >= d for d in (1, 2, 3)], -1: [chunk < 4 - d for d in (1, 2, 3)]}

    def shifted(j, d):
        return shift[j, pl.ds(16 - 2 * d, 8, stride=2), :]

    def set_shift(j, value):
        shift[j, pl.ds(16, 8, stride=2), :] = value

    zs = step_sums(dat_z)
    set_shift(12, zs[0])
    set_shift(13, zs[1])
    moved = tuple(shifted(j, d) for d in (1, 2, -1, -2) for j in (12, 13))

    def line_final(p, moved):
        ends = local_pass(p, 0, PAIRS, 2, 3, dat_z, spread_z, ztile)
        for e, parts in enumerate(ends):
            for i in range(3):
                set_shift(e * 3 + i, parts[i])
        starts = []
        for e, (k, sign) in enumerate(((2, 1), (2, -1), (3, -1), (3, 1))):
            rate = rates(k, p)
            at = 0 if sign == 1 else 4
            near, far = (moved[at], moved[at], moved[at + 1]), (moved[at + 2], moved[at + 2], moved[at + 3])
            start = []
            for i in range(3):
                f1, f2, f3 = (jnp.where(from_chunk[sign][d - 1], shifted(e * 3 + i, d * sign), 0.0)
                              for d in (1, 2, 3))
                start.append(f1 + jnp.exp2(near[i] * rate[i]) * (f2 + jnp.exp2(far[i] * rate[i]) * f3))
            starts.append(start)
        final_pass(p, 0, PAIRS, 2, 3, dat_z, spread_z, acc_z, starts)
        return moved

    lax.fori_loop(0, PAIRS, line_final, moved)
    sums = channel_sums()
    for t in range(T):
        at = pl.ds(t, 8, stride=16)
        zout[0, at, :] = acc_z[0, t]
        zout[1, at, :] = acc_z[2, t]
        zout[2, at, :] = settle(acc_z, t)
        zout[3, at, :] = sums[t]

    def send_back(i, _):
        to = lax.rem(row + i, ROWS)
        for c in range(2):
            remote(zout.at[:, pl.ds(pl.multiple_of(c * 64 + to * 8, 8), 8), :],
                   zback.at[:, pl.ds(pl.multiple_of(row * 16 + c * 8, 8), 8), :], 4, rows=to).start()
        return 0

    lax.fori_loop(1, ROWS, send_back, 0)
    for c in range(2):
        zback[:, pl.ds(pl.multiple_of(row * 16 + c * 8, 8), 8), :] = (
            zout[:, pl.ds(pl.multiple_of(c * 64 + row * 8, 8), 8), :])

    taken(brecv.at[pl.ds(0, COLS - 1)], recv_sem, 3)

    def row_final(p, _):
        starts = [[brecv[q * PAIRS + p, i] for i in range(3)] for q in range(4)]
        final_pass(p, p, p, 0, 1, dat_r, spread_r, acc_r, starts)
        return 0

    lax.fori_loop(0, PAIRS, row_final, 0)

    def send_a(i, _):
        to = lax.rem(col + i, COLS)
        remote(asend.at[to], arecv.at[col], 5, cols=to).start()
        return 0

    lax.fori_loop(1, COLS, send_a, 0)
    arecv[col] = asend[col]

    sums = channel_sums()
    for t in range(T):
        at = pl.ds(t, 8, stride=16)
        nat[0, at, :] = acc_r[0, t]
        nat[1, at, :] = acc_r[2, t]
        nat[2, at, :] = settle(acc_r, t)
        nat[3, at, :] = sums[t]

    taken(arecv.at[pl.ds(0, COLS - 1)], recv_sem, 5)
    total = arecv[0]
    for b in range(1, COLS):
        total = total + arecv[b]
    zsum[row] = total

    def send_zsum(i, _):
        to = lax.rem(row + i, ROWS)
        remote(zsum.at[row], zsum.at[row], 6, rows=to).start()
        return 0

    lax.fori_loop(1, ROWS, send_zsum, 0)
    taken(zsum.at[pl.ds(0, ROWS - 1)], recv_sem, 6)
    total = zsum[0]
    for b in range(1, ROWS):
        total = total + zsum[b]
    fin_ref[col] = total

    def send_fin(i, _):
        to = lax.rem(col + i, COLS)
        remote(fin_ref.at[col], fin_ref.at[col], 7, cols=to).start()
        return 0

    lax.fori_loop(1, COLS, send_fin, 0)

    taken(zback.at[:, pl.ds(0, 112), :], recv_sem, 4)
    for r in range(8):
        back = pl.ds(r, 16, stride=8)
        at = pl.ds(r * 16, 16)
        th_lo = nat[0, at, :] + zback[0, back, :]
        m_lo = nat[1, at, :] + zback[1, back, :]
        packed = nat[2, at, :] + zback[2, back, :]
        th_hi = packed[:, :64]
        m_hi = pltpu.roll(packed, 64, 1)[:, :64]
        xv = x_ref[r].astype(F32)
        sv = s_ref[r].astype(F32)
        gv = g_ref[r].astype(F32)
        gi_ref[r, :, :128] = sk_ref[:, :128] * gv[:, :128] + sv[:, :128] * th_lo
        gi_ref[r, :, 128:] = sk_ref[:, 128:] * gv[:, 128:] + sv[:, 128:] * th_hi
        gs_ref[r, :, :128] = th_lo * xv[:, :128] + LN2 * m_lo
        gs_ref[r, :, 128:] = th_hi * xv[:, 128:] + LN2 * m_hi
        gc_ref[r] = nat[3, at, :] + pltpu.roll(zback[3, back, :], 64, 1)

    taken(fin_ref.at[pl.ds(0, COLS - 1)], recv_sem, 7)

    taken(zrecv.at[:, pl.ds(0, 112), :], send_sem, 0)
    taken(srecv.at[pl.ds(0, COLS - 1)], send_sem, 1)
    taken(crecv.at[pl.ds(0, COLS - 1)], send_sem, 2)
    taken(brecv.at[pl.ds(0, COLS - 1)], send_sem, 3)
    taken(zback.at[:, pl.ds(0, 112), :], send_sem, 4)
    taken(arecv.at[pl.ds(0, COLS - 1)], send_sem, 5)
    taken(zsum.at[pl.ds(0, ROWS - 1)], send_sem, 6)
    taken(fin_ref.at[pl.ds(0, COLS - 1)], send_sem, 7)


def on_device(inputs, step_sizes, write_coef, read_coef, rate_table, skip_gain, grad_out):
    by_state = (rate_table * (-LOG2E)).transpose(0, 2, 1)
    lo = by_state[:, :, :128].reshape(4, 2, 8, 128)
    hi = by_state[:, :, 128:].reshape(4, 2, 8, 64)
    table = jnp.stack([lo[:, 0], lo[:, 1], jnp.concatenate([hi[:, 0], hi[:, 1]], axis=-1)], axis=2)
    vm = pl.BlockSpec(memory_space=pltpu.VMEM)
    B16 = jnp.bfloat16
    scratch = [
        pltpu.VMEM(shape, kind[0] if kind else F32)
        for shape, *kind in (
            ((6, 128, 128),),
            ((5, T, 8, 128),),
            ((T, 8, 128),),
            ((6, T, 8, 128),),
            ((6, T, 8, 128),),
            ((PAIRS + 1, T, 6, 8, 128),),
            ((2, 8, 128),),
            ((COLS, 2, 8, 128),),
            ((COLS, 3, 8, 128),),
            ((COLS, 3, 8, 128),),
            ((COLS, 3, 8, 128),),
            ((COLS, 3, 8, 128),),
            ((5, 128, 128),),
            ((128, 128), B16),
            ((T, 8, 8, 128),),
            ((4, T, 8, 128),),
            ((4, T, 8, 128),),
            ((4, PAIRS, 2, T, 8, 128),),
            ((PAIRS, 128, 12 * 128), B16),
            ((4, PAIRS * 256, 128), B16),
            ((PAIRS, 128, 12 * 128),),
            ((1, 128, 12 * 128),),
            ((14, 40, 128),),
            ((4, 128, 128),),
            ((4, 128, 128),),
            ((4, 128, 128),),
            ((COLS, 8, 128),),
            ((COLS, 8, 128),),
            ((ROWS, 8, 128),),
        )
    ]
    scratch += [pltpu.SemaphoreType.DMA((8,)), pltpu.SemaphoreType.DMA((8,))]
    gi, gs, gc, fin = pl.pallas_call(
        body,
        out_shape=[
            jax.ShapeDtypeStruct((8, 16, 192), F32),
            jax.ShapeDtypeStruct((8, 16, 192), F32),
            jax.ShapeDtypeStruct((8, 16, 128), F32),
            jax.ShapeDtypeStruct((COLS, 8, 128), F32),
        ],
        in_specs=[vm] * 7,
        out_specs=[vm] * 4,
        scratch_shapes=scratch,
        compiler_params=pltpu.CompilerParams(
            collective_id=0, has_side_effects=True, vmem_limit_bytes=48 * 1024 * 1024),
    )(inputs, step_sizes, grad_out, write_coef, read_coef, table, skip_gain.reshape(1, 192))
    parts = fin.reshape(4, 8, 8, 128)
    lo = parts[:, :, :2].transpose(0, 3, 2, 1).reshape(4, 128, 16)
    hi = parts[:, :, 2].reshape(4, 8, 2, 64).transpose(0, 3, 2, 1).reshape(4, 64, 16)
    grad_rates = jnp.concatenate([lo, hi], axis=1)
    grad_skip = jnp.concatenate([fin[0, 3], fin[0, 4, :64]])
    kinds = gc.reshape(8, 16, 2, 2, 2, 16).transpose(3, 2, 4, 0, 1, 5).reshape(2, 4, 8, 16, 16)
    return gi, gs, kinds[0], kinds[1], grad_rates, grad_skip


def solution(mesh):
    cells, coefs = P("rows", "cols", None), P(None, "rows", "cols", None)
    return jax.shard_map(
        on_device, mesh=mesh, in_specs=(cells, cells, coefs, coefs, P(), P(), cells),
        out_specs=(cells, cells, coefs, coefs, P(), P()), check_vma=False)
```

```python
import functools
import math

import jax
import jax.numpy as jnp
from jax import lax
from jax.experimental import pallas as pl
from jax.experimental.pallas import tpu as pltpu
from jax.sharding import PartitionSpec as P

F32 = jnp.float32
T = 16
PAIRS = 8
LOG2E = 1.4426950408889634
LN2 = 0.6931471805599453
COLS = 32
ROWS = 8


def low_half():
    return lax.broadcasted_iota(jnp.int32, (8, 128), 1) < 64


def fold(q, low):
    return jnp.where(low, q[0], q[1]) + q[2], jnp.where(low, q[1], q[0])


def tri(f, *groups):
    return [f(*parts) for parts in zip(*groups)]


def add(a, b):
    return a + b


def mul(a, b):
    return a * b


def body(x_in, s_in, g_in, w_in, r_in, rate_in, sk_in,
         gi_out, gs_out, gw_out, gr_out, rate_out, skip_out,
         gi_ref, gs_ref, gw_ref, gr_ref, rate_sum, skip_sum, fin_ref,
         x_ref, s_ref, g_ref, w_ref, r_ref, rate_ref, sk_ref, rt_ref,
         flat, zmsg, rowtile, dat_r, dat_z, decays, ssend, srecv, csend, crecv, bsend, brecv,
         zrecv, ztile, keep, acc_r, acc_z, zbuf_r, zbuf_z, pick, place, spread_r, spread_z, shift, nat,
         zout, zback, asend, arecv, zsum, send_sem, recv_sem, in_sem, out_sem):
    entries = [pltpu.make_async_copy(src, dst, in_sem.at[i]) for i, (src, dst) in enumerate(
        ((x_in, x_ref), (s_in, s_ref), (g_in, g_ref), (w_in, w_ref), (r_in, r_ref), (rate_in, rate_ref), (sk_in, sk_ref)))]
    for entry in entries:
        entry.start()
    col = lax.axis_index("cols")
    row = lax.axis_index("rows")
    low = low_half()

    barrier = pltpu.get_barrier_semaphore()

    def greet_cols(i, _):
        pl.semaphore_signal(barrier, inc=1, device_id={"cols": lax.rem(col + i, COLS)},
                            device_id_type=pl.DeviceIdType.MESH)
        return 0

    def greet_rows(i, _):
        pl.semaphore_signal(barrier, inc=1, device_id={"rows": lax.rem(row + i, ROWS)},
                            device_id_type=pl.DeviceIdType.MESH)
        return 0

    lax.fori_loop(1, COLS, greet_cols, 0)
    lax.fori_loop(1, ROWS, greet_rows, 0)

    def remote(src, dst, n, **to):
        return pltpu.make_async_remote_copy(
            src_ref=src, dst_ref=dst, send_sem=send_sem.at[n], recv_sem=recv_sem.at[n],
            device_id=to, device_id_type=pl.DeviceIdType.MESH)

    def taken(ref, sem, n):
        pltpu.make_async_copy(ref, ref, sem.at[n]).wait()

    for entry in entries:
        entry.wait()
    for r in range(8):
        sv = s_ref[r].astype(F32)
        gv = g_ref[r].astype(F32)
        pv = sv * x_ref[r].astype(F32)
        at = pl.ds(r * 16, 16)
        flat[0, at, :] = sv[:, :128]
        flat[1, at, :] = pv[:, :128]
        flat[2, at, :] = gv[:, :128]
        flat[3, at, :] = jnp.concatenate([sv[:, 128:], pv[:, 128:]], axis=1)
        flat[4, at, :] = jnp.concatenate(
            [ref[k, r].astype(F32) for ref in (w_ref, r_ref) for k in (2, 3)] + [gv[:, 128:]], axis=1)
        flat[5, at, :] = jnp.concatenate(
            [ref[k, r].astype(F32) for ref in (w_ref, r_ref) for k in (0, 1)] + [gv[:, 128:]], axis=1)

    for t in range(T):
        at = pl.ds(t, 8, stride=16)
        for q in range(5):
            zmsg[q, t] = flat[q, at, :]
        rowtile[t] = flat[5, at, :]

    def unpack(dat, t, tiles):
        s_lo, p_lo, g_lo, sp, gc = tiles
        spr = pltpu.roll(sp, 64, 1)
        dat[0, t] = s_lo
        dat[1, t] = jnp.where(low, sp, spr)
        dat[2, t] = p_lo
        dat[3, t] = jnp.where(low, spr, sp)
        dat[4, t] = g_lo
        dat[5, t] = jnp.where(low, pltpu.roll(gc, 64, 1), gc)

    def step_sums(dat):
        lo, hi = dat[0, 0], dat[1, 0]
        for t in range(1, T):
            lo, hi = lo + dat[0, t], hi + dat[1, t]
        return lo, hi

    pl.semaphore_wait(barrier, COLS - 1 + ROWS - 1)

    def send_z(i, _):
        to = lax.rem(row + i, ROWS)
        for c in range(2):
            remote(zmsg.at[:, 2 * to + c],
                   zrecv.at[:, pl.ds(pl.multiple_of(c * 64 + row * 8, 8), 8), :], 0, rows=to).start()
        return 0

    lax.fori_loop(1, ROWS, send_z, 0)
    for c in range(2):
        for q in range(5):
            zrecv[q, pl.ds(pl.multiple_of(c * 64 + row * 8, 8), 8), :] = zmsg[q, 2 * row + c]

    for t in range(T):
        unpack(dat_r, t, (zmsg[0, t], zmsg[1, t], zmsg[2, t], zmsg[3, t], rowtile[t]))
    ssum = step_sums(dat_r)
    ssend[0] = ssum[0]
    ssend[1] = ssum[1]
    srecv[col] = ssend[...]

    def send_s(i, _):
        to = lax.rem(col + i, COLS)
        remote(ssend, srecv.at[col], 1, cols=to).start()
        return 0

    lax.fori_loop(1, COLS, send_s, 0)

    pick_j = lax.broadcasted_iota(jnp.int32, (64, 128), 0)
    pick_up = pick_j - jnp.where(lax.broadcasted_iota(jnp.int32, (64, 128), 1) < 64, 0, 8)

    def fill_pick(p, _):
        for which in range(4):
            base = 16 * which
            for i, (source, start) in enumerate(((pick_j, base), (pick_j, base + 8), (pick_up, base))):
                pick[p, :, pl.ds((which * 3 + i) * 128, 128)] = jnp.where(
                    source == start + p, 1.0, 0.0).astype(jnp.bfloat16)
        return 0

    lax.fori_loop(0, PAIRS, fill_pick, 0)

    for k in range(4):
        early, late = rate_ref[k, :8] * -LOG2E, rate_ref[k, 8:] * -LOG2E
        rt_ref[k, 0] = early[:, :128]
        rt_ref[k, 1] = late[:, :128]
        rt_ref[k, 2] = jnp.concatenate([early[:, 128:], late[:, 128:]], axis=1)

    def rates(k, p):
        return [jnp.broadcast_to(rt_ref[k, i, pl.ds(p, 1), :], (8, 128)) for i in range(3)]

    def load(dat, q, t):
        lo = dat[2 * q, t]
        return [lo, lo, dat[2 * q + 1, t]]

    W_A, W_D, R_A, R_D = 0, 1, 2, 3
    zero3 = [jnp.zeros((8, 128), F32)] * 3

    def coefs(wide, slot, t, which):
        return [wide[slot, pl.ds(t * 8, 8), pl.ds((which * 3 + i) * 128, 128)] for i in range(3)]

    def held(t, slot):
        return [decays[slot, t, i] for i in range(3)], [decays[slot, t, 3 + i] for i in range(3)]

    def local_pass(p, slot, dslot, ka, kd, dat, wide, tile):
        wide[slot] = jnp.dot(tile[:, :64], pick[p], preferred_element_type=F32)
        ra, rd = rates(ka, p), rates(kd, p)

        def up(t, carry):
            fa, md = carry[:3], carry[3:]
            s = load(dat, 0, t)
            da = tri(lambda a, b: jnp.exp2(a * b), s, ra)
            dd = tri(lambda a, b: jnp.exp2(a * b), s, rd)
            for i in range(3):
                decays[dslot, t, i] = da[i]
                decays[dslot, t, 3 + i] = dd[i]
            drive = tri(mul, load(dat, 1, t), coefs(wide, slot, t, W_A))
            fa = tri(add, tri(mul, da, fa), drive)
            md = tri(mul, dd, tri(add, tri(mul, load(dat, 2, t), coefs(wide, slot, t, R_D)), md))
            return (*fa, *md)

        def down(i, carry):
            t = T - 1 - i
            ma, fd = carry[:3], carry[3:]
            da, dd = held(t, dslot)
            drive = tri(mul, load(dat, 1, t), coefs(wide, slot, t, W_D))
            fd = tri(add, tri(mul, dd, fd), drive)
            ma = tri(mul, da, tri(add, tri(mul, load(dat, 2, t), coefs(wide, slot, t, R_A)), ma))
            return (*ma, *fd)

        a = lax.fori_loop(0, T, up, (*zero3, *zero3), unroll=True)
        b = lax.fori_loop(0, T, down, (*zero3, *zero3), unroll=True)
        return a[:3], b[:3], b[3:], a[3:]

    def final_pass(p, slot, dslot, ka, kd, dat, wide, acc, zbuf, starts):
        ra, rd = rates(ka, p), rates(kd, p)
        fa0, ma0, fd0, md0 = starts

        def put(q, t, parts):
            zbuf[q, p, 0, t], zbuf[q, p, 1, t] = fold(parts, low)

        def up(t, carry):
            h, m = carry[:3], carry[3:]
            da, dd = held(t, dslot)
            sx, g = load(dat, 1, t), load(dat, 2, t)
            db = tri(mul, da, h)
            h = tri(add, db, tri(mul, sx, coefs(wide, slot, t, W_A)))
            adj = tri(add, tri(mul, g, coefs(wide, slot, t, R_D)), m)
            for i in range(3):
                keep[t, i] = db[i]
                keep[t, 3 + i] = adj[i]
            put(2, t, tri(mul, h, g))
            put(1, t, tri(mul, adj, sx))
            th = tri(mul, adj, coefs(wide, slot, t, W_D))
            keep[t, 6] = th[0] + th[1]
            keep[t, 7] = th[2]
            return (*h, *tri(mul, dd, adj))

        def down(i, carry):
            t = T - 1 - i
            m, h, acc_a, acc_d = carry[:3], carry[3:6], carry[6:9], carry[9:]
            da, dd = held(t, dslot)
            s, sx, g = load(dat, 0, t), load(dat, 1, t), load(dat, 2, t)
            db = tri(mul, dd, h)
            h = tri(add, db, tri(mul, sx, coefs(wide, slot, t, W_D)))
            adj = tri(add, tri(mul, g, coefs(wide, slot, t, R_A)), m)
            put(3, t, tri(mul, h, g))
            put(0, t, tri(mul, adj, sx))
            th = tri(mul, adj, coefs(wide, slot, t, W_A))
            acc[0, t] += keep[t, 6] + (th[0] + th[1])
            acc[1, t] += keep[t, 7] + th[2]
            mem_a = tri(mul, adj, [keep[t, i] for i in range(3)])
            mem_d = tri(mul, [keep[t, 3 + i] for i in range(3)], db)
            mr = tri(add, tri(mul, mem_a, ra), tri(mul, mem_d, rd))
            acc[2, t] += mr[0] + mr[1]
            acc[3, t] += mr[2]
            acc_a = tri(add, acc_a, tri(mul, mem_a, s))
            acc_d = tri(add, acc_d, tri(mul, mem_d, s))
            return (*tri(mul, da, adj), *h, *acc_a, *acc_d)

        lax.fori_loop(0, T, up, (*fa0, *md0), unroll=True)
        out = lax.fori_loop(0, T, down, (*ma0, *fd0, *zero3, *zero3), unroll=True)
        for k, sums in ((ka, out[6:9]), (kd, out[9:])):
            for i in range(3):
                asend[k * PAIRS + p, pl.ds(i, 1), :] = -jnp.sum(sums[i], axis=0, keepdims=True)

    def channel_sums(zbuf):
        total = None
        for q in range(4):
            whole = jnp.concatenate(
                [zbuf[q, p, j].reshape(128, 128) for p in range(PAIRS) for j in range(2)], axis=1)
            high = whole.astype(jnp.bfloat16)
            rest = (whole - high.astype(F32)).astype(jnp.bfloat16)
            part = jnp.dot(high, place[q], preferred_element_type=F32)
            part = part + jnp.dot(rest, place[q], preferred_element_type=F32)
            total = part if total is None else total + part
        return total.reshape(T, 8, 128)

    def settle(acc, t):
        th, m = acc[1, t], acc[3, t]
        return jnp.where(low, th, m) + pltpu.roll(jnp.where(low, m, th), 64, 1)

    tile_r = rowtile[...].reshape(128, 128).astype(jnp.bfloat16)
    ztile[...] = tile_r

    def row_local(p, _):
        fa, ma, fd, md = local_pass(p, p, p, 0, 1, dat_r, spread_r, ztile)
        for q, parts in enumerate((fa, ma, fd, md)):
            for i in range(3):
                csend[q * PAIRS + p, i] = parts[i]
        return 0

    lax.fori_loop(0, PAIRS, row_local, 0, unroll=2)

    def send_c(i, _):
        to = lax.rem(col + i, COLS)
        remote(csend.at[to], crecv.at[col], 2, cols=to).start()
        return 0

    lax.fori_loop(1, COLS, send_c, 0)
    crecv[col] = csend[col]

    place_k = lax.broadcasted_iota(jnp.int32, (128, 128), 0) // 64 * 8
    place_n = lax.broadcasted_iota(jnp.int32, (128, 128), 1)

    def fill_place(p, _):
        for q in range(4):
            for j, source in enumerate((place_n - place_k, place_n + place_k - 8)):
                place[q, pl.ds(pl.multiple_of(p * 256 + j * 128, 128), 128), :] = jnp.where(
                    source == 16 * q + p, 1.0, 0.0).astype(jnp.bfloat16)
        return 0

    lax.fori_loop(0, PAIRS, fill_place, 0)
    skip = jnp.zeros((1, 192), F32)
    for r in range(8):
        skip = skip + jnp.sum(g_ref[r].astype(F32) * x_ref[r].astype(F32), axis=0, keepdims=True)
    skip_lo = skip[:, :128]
    skip_hi = jnp.concatenate([skip[:, 128:], skip[:, 128:]], axis=1)
    skip_tile = jnp.concatenate([jnp.zeros((3, 128), F32), skip_lo, skip_hi, jnp.zeros((3, 128), F32)], axis=0)

    def put_skip(o, _):
        asend[o] = skip_tile
        return 0

    lax.fori_loop(0, COLS, put_skip, 0)
    acc_r[...] = jnp.zeros_like(acc_r)
    acc_z[...] = jnp.zeros_like(acc_z)
    shift[...] = jnp.zeros_like(shift)

    taken(srecv.at[pl.ds(0, COLS - 1)], recv_sem, 1)
    taken(crecv.at[pl.ds(0, COLS - 1)], recv_sem, 2)
    kind = col // PAIRS
    pair = lax.rem(col, PAIRS)
    falls = jnp.where((kind == 1) | (kind == 2), 1, 0)
    own_rates = rates(kind // 2, pair)

    def chain(i, carry):
        b = i + falls * (COLS - 1 - 2 * i)
        for j in range(3):
            bsend[b, j] = carry[j]
        s_lo, s_hi = srecv[b, 0], srecv[b, 1]
        kept = tri(lambda a, r: jnp.exp2(a * r), [s_lo, s_lo, s_hi], own_rates)
        return tuple(kept[j] * carry[j] + crecv[b, j] for j in range(3))

    lax.fori_loop(0, COLS, chain, tuple(zero3), unroll=True)

    def send_b(i, _):
        to = lax.rem(col + i, COLS)
        remote(bsend.at[to], brecv.at[col], 3, cols=to).start()
        return 0

    lax.fori_loop(1, COLS, send_b, 0)
    brecv[col] = bsend[col]

    taken(zrecv.at[:, pl.ds(0, 112), :], recv_sem, 0)
    for t in range(T):
        at = pl.ds(t, 8, stride=16)
        tiles = [zrecv[q, at, :] for q in range(5)]
        unpack(dat_z, t, tiles)
        rowtile[t] = tiles[4]
    ztile[...] = rowtile[...].reshape(128, 128).astype(jnp.bfloat16)
    chunk = lax.rem(lax.broadcasted_iota(jnp.int32, (8, 128), 0), 4)
    from_chunk = {1: [chunk >= d for d in (1, 2, 3)], -1: [chunk < 4 - d for d in (1, 2, 3)]}

    def shifted(j, d):
        return shift[j, pl.ds(16 - 2 * d, 8, stride=2), :]

    def set_shift(j, value):
        shift[j, pl.ds(16, 8, stride=2), :] = value

    zs = step_sums(dat_z)
    set_shift(12, zs[0])
    set_shift(13, zs[1])
    moved = tuple(shifted(j, d) for d in (1, 2, -1, -2) for j in (12, 13))

    def line_final(p, moved):
        ends = local_pass(p, 0, PAIRS, 2, 3, dat_z, spread_z, ztile)
        for e, parts in enumerate(ends):
            for i in range(3):
                set_shift(e * 3 + i, parts[i])
        starts = []
        for e, (k, sign) in enumerate(((2, 1), (2, -1), (3, -1), (3, 1))):
            rate = rates(k, p)
            at = 0 if sign == 1 else 4
            near, far = (moved[at], moved[at], moved[at + 1]), (moved[at + 2], moved[at + 2], moved[at + 3])
            start = []
            for i in range(3):
                f1, f2, f3 = (jnp.where(from_chunk[sign][d - 1], shifted(e * 3 + i, d * sign), 0.0)
                              for d in (1, 2, 3))
                start.append(f1 + jnp.exp2(near[i] * rate[i]) * (f2 + jnp.exp2(far[i] * rate[i]) * f3))
            starts.append(start)
        final_pass(p, 0, PAIRS, 2, 3, dat_z, spread_z, acc_z, zbuf_z, starts)
        return moved

    lax.fori_loop(0, PAIRS, line_final, moved, unroll=2)
    taken(brecv.at[pl.ds(0, COLS - 1)], recv_sem, 3)

    def row_final(p, _):
        starts = [[brecv[q * PAIRS + p, i] for i in range(3)] for q in range(4)]
        final_pass(p, p, p, 0, 1, dat_r, spread_r, acc_r, zbuf_r, starts)
        return 0

    lax.fori_loop(0, PAIRS, row_final, 0, unroll=2)

    def send_a(i, _):
        to = lax.rem(col + i, COLS)
        remote(asend.at[to], arecv.at[col], 5, cols=to).start()
        return 0

    lax.fori_loop(1, COLS, send_a, 0)
    arecv[col] = asend[col]

    sums = channel_sums(zbuf_z)
    for t in range(T):
        at = pl.ds(t, 8, stride=16)
        zout[0, at, :] = acc_z[0, t]
        zout[1, at, :] = acc_z[2, t]
        zout[2, at, :] = settle(acc_z, t)
        zout[3, at, :] = sums[t]

    def send_back(i, _):
        to = lax.rem(row + i, ROWS)
        for c in range(2):
            remote(zout.at[:, pl.ds(pl.multiple_of(c * 64 + to * 8, 8), 8), :],
                   zback.at[:, pl.ds(pl.multiple_of(row * 16 + c * 8, 8), 8), :], 4, rows=to).start()
        return 0

    lax.fori_loop(1, ROWS, send_back, 0)
    for c in range(2):
        zback[:, pl.ds(pl.multiple_of(row * 16 + c * 8, 8), 8), :] = (
            zout[:, pl.ds(pl.multiple_of(c * 64 + row * 8, 8), 8), :])

    taken(arecv.at[pl.ds(0, COLS - 1)], recv_sem, 5)
    total = arecv[0]
    for b in range(1, COLS):
        total = total + arecv[b]
    zsum[row] = total

    def send_zsum(i, _):
        to = lax.rem(row + i, ROWS)
        remote(zsum.at[row], zsum.at[row], 6, rows=to).start()
        return 0

    lax.fori_loop(1, ROWS, send_zsum, 0)

    sums = channel_sums(zbuf_r)
    for t in range(T):
        at = pl.ds(t, 8, stride=16)
        nat[0, at, :] = acc_r[0, t]
        nat[1, at, :] = acc_r[2, t]
        nat[2, at, :] = settle(acc_r, t)
        nat[3, at, :] = sums[t]

    taken(zsum.at[pl.ds(0, ROWS - 1)], recv_sem, 6)
    total = zsum[0]
    for b in range(1, ROWS):
        total = total + zsum[b]
    fin_ref[col] = total

    def send_fin(i, _):
        to = lax.rem(col + i, COLS)
        remote(fin_ref.at[col], fin_ref.at[col], 7, cols=to).start()
        return 0

    lax.fori_loop(1, COLS, send_fin, 0)

    taken(zback.at[:, pl.ds(0, 112), :], recv_sem, 4)
    for r in range(8):
        back = pl.ds(r, 16, stride=8)
        at = pl.ds(r * 16, 16)
        th_lo = nat[0, at, :] + zback[0, back, :]
        m_lo = nat[1, at, :] + zback[1, back, :]
        packed = nat[2, at, :] + zback[2, back, :]
        th_hi = packed[:, :64]
        m_hi = pltpu.roll(packed, 64, 1)[:, :64]
        xv = x_ref[r].astype(F32)
        sv = s_ref[r].astype(F32)
        gv = g_ref[r].astype(F32)
        gi_ref[r, :, :128] = sk_ref[:, :128] * gv[:, :128] + sv[:, :128] * th_lo
        gi_ref[r, :, 128:] = sk_ref[:, 128:] * gv[:, 128:] + sv[:, 128:] * th_hi
        gs_ref[r, :, :128] = th_lo * xv[:, :128] + LN2 * m_lo
        gs_ref[r, :, 128:] = th_hi * xv[:, 128:] + LN2 * m_hi
        for first, sums in ((0, nat[3, at, :]), (2, zback[3, back, :])):
            for j in range(2):
                gw_ref[first + j, r] = sums[:, 16 * j : 16 * j + 16]
                gr_ref[first + j, r] = sums[:, 32 + 16 * j : 48 + 16 * j]

    leaving = [pltpu.make_async_copy(src, dst, out_sem.at[i]) for i, (src, dst) in enumerate(
        ((gi_ref, gi_out), (gs_ref, gs_out), (gw_ref, gw_out), (gr_ref, gr_out)))]
    for copy in leaving:
        copy.start()

    taken(fin_ref.at[pl.ds(0, COLS - 1)], recv_sem, 7)
    for k in range(4):
        lo, late, hi = (jnp.concatenate([fin_ref[k * PAIRS + p, pl.ds(i, 1), :] for p in range(PAIRS)], axis=0)
                        for i in range(3))
        rate_sum[k, :8, :128] = lo
        rate_sum[k, 8:, :128] = late
        rate_sum[k, :8, 128:] = hi[:, :64]
        rate_sum[k, 8:, 128:] = hi[:, 64:]
    skip_sum[:, :128] = fin_ref[0, 3:4, :]
    skip_sum[:, 128:] = fin_ref[0, 4:5, :64]
    last = [pltpu.make_async_copy(rate_sum, rate_out, out_sem.at[4]),
            pltpu.make_async_copy(skip_sum, skip_out, out_sem.at[5])]
    for copy in last:
        copy.start()

    taken(zrecv.at[:, pl.ds(0, 112), :], send_sem, 0)
    taken(srecv.at[pl.ds(0, COLS - 1)], send_sem, 1)
    taken(crecv.at[pl.ds(0, COLS - 1)], send_sem, 2)
    taken(brecv.at[pl.ds(0, COLS - 1)], send_sem, 3)
    taken(zback.at[:, pl.ds(0, 112), :], send_sem, 4)
    taken(arecv.at[pl.ds(0, COLS - 1)], send_sem, 5)
    taken(zsum.at[pl.ds(0, ROWS - 1)], send_sem, 6)
    taken(fin_ref.at[pl.ds(0, COLS - 1)], send_sem, 7)
    for copy in leaving + last:
        copy.wait()


def leave(*refs):
    ins, outs, held, sems = refs[:6], refs[6:12], refs[12:18], refs[18]
    arrive = [pltpu.make_async_copy(ins[i], held[i], sems.at[i]) for i in range(6)]
    depart = [pltpu.make_async_copy(held[i], outs[i], sems.at[6 + i]) for i in range(6)]
    for copy in arrive:
        copy.start()
    for i in range(6):
        arrive[i].wait()
        depart[i].start()
    for copy in depart:
        copy.wait()


def on_device(inputs, step_sizes, write_coef, read_coef, rate_table, skip_gain, grad_out):
    B16 = jnp.bfloat16
    scratch = [
        pltpu.VMEM(shape, kind[0] if kind else F32)
        for shape, *kind in (
            ((8, 16, 192),),
            ((8, 16, 192),),
            ((4, 8, 16, 16),),
            ((4, 8, 16, 16),),
            ((4, 16, 192),),
            ((1, 192),),
            ((COLS, 8, 128),),
            ((8, 16, 192), B16),
            ((8, 16, 192), B16),
            ((8, 16, 192), B16),
            ((4, 8, 16, 16), B16),
            ((4, 8, 16, 16), B16),
            ((4, 16, 192),),
            ((1, 192),),
            ((4, 3, PAIRS, 128),),
            ((6, 128, 128),),
            ((5, T, 8, 128),),
            ((T, 8, 128),),
            ((6, T, 8, 128),),
            ((6, T, 8, 128),),
            ((PAIRS + 1, T, 6, 8, 128),),
            ((2, 8, 128),),
            ((COLS, 2, 8, 128),),
            ((COLS, 3, 8, 128),),
            ((COLS, 3, 8, 128),),
            ((COLS, 3, 8, 128),),
            ((COLS, 3, 8, 128),),
            ((5, 128, 128),),
            ((128, 128), B16),
            ((T, 8, 8, 128),),
            ((4, T, 8, 128),),
            ((4, T, 8, 128),),
            ((4, PAIRS, 2, T, 8, 128),),
            ((4, PAIRS, 2, T, 8, 128),),
            ((PAIRS, 64, 12 * 128), B16),
            ((4, PAIRS * 256, 128), B16),
            ((PAIRS, 128, 12 * 128),),
            ((1, 128, 12 * 128),),
            ((14, 40, 128),),
            ((4, 128, 128),),
            ((4, 128, 128),),
            ((4, 128, 128),),
            ((COLS, 8, 128),),
            ((COLS, 8, 128),),
            ((ROWS, 8, 128),),
        )
    ]
    scratch += [pltpu.SemaphoreType.DMA((8,)), pltpu.SemaphoreType.DMA((8,)), pltpu.SemaphoreType.DMA((7,)), pltpu.SemaphoreType.DMA((6,))]
    cells = jax.ShapeDtypeStruct((8, 16, 192), F32)
    kinds = jax.ShapeDtypeStruct((4, 8, 16, 16), F32)
    shapes = [cells, cells, kinds, kinds, jax.ShapeDtypeStruct((4, 16, 192), F32), jax.ShapeDtypeStruct((1, 192), F32)]
    hbm = pl.BlockSpec(memory_space=pltpu.MemorySpace.HBM)
    made = pl.pallas_call(
        body,
        out_shape=shapes,
        in_specs=[hbm] * 7,
        out_specs=[hbm] * 6,
        scratch_shapes=scratch,
        compiler_params=pltpu.CompilerParams(
            collective_id=0, has_side_effects=True, vmem_limit_bytes=60 * 1024 * 1024),
    )(inputs, step_sizes, grad_out, write_coef, read_coef, rate_table.transpose(0, 2, 1), skip_gain.reshape(1, 192))
    gi, gs, gw, gr, rate, skip = pl.pallas_call(
        leave,
        out_shape=shapes,
        in_specs=[hbm] * 6,
        out_specs=[hbm] * 6,
        scratch_shapes=[pltpu.VMEM(a.shape, F32) for a in shapes] + [pltpu.SemaphoreType.DMA((12,))],
        compiler_params=pltpu.CompilerParams(vmem_limit_bytes=60 * 1024 * 1024),
    )(*made)
    return gi, gs, gw, gr, rate.transpose(0, 2, 1), skip.reshape(192)


def solution(mesh):
    cells, coefs = P("rows", "cols", None), P(None, "rows", "cols", None)
    return jax.shard_map(
        on_device, mesh=mesh, in_specs=(cells, cells, coefs, coefs, P(), P(), cells),
        out_specs=(cells, cells, coefs, coefs, P(), P()), check_vma=False)
```

```python
import functools
import math

import jax
import jax.numpy as jnp
from jax import lax
from jax.experimental import pallas as pl
from jax.experimental.pallas import tpu as pltpu
from jax.sharding import PartitionSpec as P

F32 = jnp.float32
T = 16
PAIRS = 8
LOG2E = 1.4426950408889634
LN2 = 0.6931471805599453
COLS = 32
ROWS = 8


def low_half():
    return lax.broadcasted_iota(jnp.int32, (8, 128), 1) < 64


def fold(q, low):
    return jnp.where(low, q[0], q[1]) + q[2], jnp.where(low, q[1], q[0])


def tri(f, *groups):
    return [f(*parts) for parts in zip(*groups)]


def tree(parts):
    while len(parts) > 1:
        parts = [a + b for a, b in zip(parts[::2], parts[1::2])]
    return parts[0]


def add(a, b):
    return a + b


def mul(a, b):
    return a * b


def body(x_in, s_in, g_in, w_in, r_in, rate_in, sk_in,
         gi_out, gs_out, gw_out, gr_out, rate_out, skip_out,
         gi_ref, gs_ref, gw_ref, gr_ref, rate_sum, skip_sum, fin_ref,
         x_ref, s_ref, g_ref, w_ref, r_ref, rate_ref, sk_ref, rt_ref,
         flat, zmsg, rowtile, dat_r, dat_z, decays, ssend, srecv, csend, crecv, bsend, brecv,
         zrecv, ztile, keep, acc_r, acc_z, zbuf_r, zbuf_z, pick, place, spread_r, spread_z, shift, nat,
         zout, zback, asend, arecv, zsum, send_sem, recv_sem, in_sem, out_sem):
    entries = [pltpu.make_async_copy(src, dst, in_sem.at[i]) for i, (src, dst) in enumerate(
        ((x_in, x_ref), (s_in, s_ref), (g_in, g_ref), (w_in, w_ref), (r_in, r_ref), (rate_in, rate_ref), (sk_in, sk_ref)))]
    for entry in entries:
        entry.start()
    col = lax.axis_index("cols")
    row = lax.axis_index("rows")
    low = low_half()

    barrier = pltpu.get_barrier_semaphore()

    def greet_cols(i, _):
        pl.semaphore_signal(barrier, inc=1, device_id={"cols": lax.rem(col + i, COLS)},
                            device_id_type=pl.DeviceIdType.MESH)
        return 0

    def greet_rows(i, _):
        pl.semaphore_signal(barrier, inc=1, device_id={"rows": lax.rem(row + i, ROWS)},
                            device_id_type=pl.DeviceIdType.MESH)
        return 0

    lax.fori_loop(1, COLS, greet_cols, 0)
    lax.fori_loop(1, ROWS, greet_rows, 0)

    def remote(src, dst, n, **to):
        return pltpu.make_async_remote_copy(
            src_ref=src, dst_ref=dst, send_sem=send_sem.at[n], recv_sem=recv_sem.at[n],
            device_id=to, device_id_type=pl.DeviceIdType.MESH)

    def taken(ref, sem, n):
        pltpu.make_async_copy(ref, ref, sem.at[n]).wait()

    for entry in entries:
        entry.wait()
    for r in range(8):
        sv = s_ref[r].astype(F32)
        gv = g_ref[r].astype(F32)
        pv = sv * x_ref[r].astype(F32)
        at = pl.ds(r * 16, 16)
        flat[0, at, :] = sv[:, :128]
        flat[1, at, :] = pv[:, :128]
        flat[2, at, :] = gv[:, :128]
        flat[3, at, :] = jnp.concatenate([sv[:, 128:], pv[:, 128:]], axis=1)

    def to_lanes(width, start):
        r = lax.broadcasted_iota(jnp.int32, (width, 128), 0)
        c = lax.broadcasted_iota(jnp.int32, (width, 128), 1)
        return jnp.where(c == r + start, 1.0, 0.0).astype(jnp.bfloat16)

    upper = jnp.dot(g_ref[:, :, 128:].reshape(128, 64), to_lanes(64, 64), preferred_element_type=F32)
    for q, first in ((4, 2), (5, 0)):
        tile = upper
        for which, (ref, k) in enumerate((ref, first + j) for ref in (w_ref, r_ref) for j in range(2)):
            tile = tile + jnp.dot(ref[k].reshape(128, 16), to_lanes(16, 16 * which), preferred_element_type=F32)
        flat[q] = tile

    for t in range(T):
        at = pl.ds(t, 8, stride=16)
        for q in range(5):
            zmsg[q, t] = flat[q, at, :]
        rowtile[t] = flat[5, at, :]

    def unpack(dat, t, tiles):
        s_lo, p_lo, g_lo, sp, gc = tiles
        spr = pltpu.roll(sp, 64, 1)
        dat[0, t] = s_lo
        dat[1, t] = jnp.where(low, sp, spr)
        dat[2, t] = p_lo
        dat[3, t] = jnp.where(low, spr, sp)
        dat[4, t] = g_lo
        dat[5, t] = jnp.where(low, pltpu.roll(gc, 64, 1), gc)

    def step_sums(dat):
        lo, hi = dat[0, 0], dat[1, 0]
        for t in range(1, T):
            lo, hi = lo + dat[0, t], hi + dat[1, t]
        return lo, hi

    pl.semaphore_wait(barrier, COLS - 1 + ROWS - 1)

    def send_z(i, _):
        to = lax.rem(row + i, ROWS)
        for c in range(2):
            remote(zmsg.at[:, 2 * to + c],
                   zrecv.at[:, pl.ds(pl.multiple_of(c * 64 + row * 8, 8), 8), :], 0, rows=to).start()
        return 0

    lax.fori_loop(1, ROWS, send_z, 0)
    for c in range(2):
        for q in range(5):
            zrecv[q, pl.ds(pl.multiple_of(c * 64 + row * 8, 8), 8), :] = zmsg[q, 2 * row + c]

    s_lo, sp = zmsg[0, 0], zmsg[3, 0]
    for t in range(1, T):
        s_lo, sp = s_lo + zmsg[0, t], sp + zmsg[3, t]
    ssend[0] = s_lo
    ssend[1] = jnp.where(low, sp, pltpu.roll(sp, 64, 1))
    srecv[col] = ssend[...]

    def send_s(i, _):
        to = lax.rem(col + i, COLS)
        remote(ssend, srecv.at[col], 1, cols=to).start()
        return 0

    lax.fori_loop(1, COLS, send_s, 0)
    for t in range(T):
        unpack(dat_r, t, (zmsg[0, t], zmsg[1, t], zmsg[2, t], zmsg[3, t], rowtile[t]))

    pick_j = lax.broadcasted_iota(jnp.int32, (64, 128), 0)
    pick_up = pick_j - jnp.where(lax.broadcasted_iota(jnp.int32, (64, 128), 1) < 64, 0, 8)

    def fill_pick(p, _):
        for which in range(4):
            base = 16 * which
            for i, (source, start) in enumerate(((pick_j, base), (pick_j, base + 8), (pick_up, base))):
                pick[p, :, pl.ds((which * 3 + i) * 128, 128)] = jnp.where(
                    source == start + p, 1.0, 0.0).astype(jnp.bfloat16)
        return 0

    lax.fori_loop(0, PAIRS, fill_pick, 0)

    for k in range(4):
        early, late = rate_ref[k, :8] * -LOG2E, rate_ref[k, 8:] * -LOG2E
        rt_ref[k, 0] = early[:, :128]
        rt_ref[k, 1] = late[:, :128]
        rt_ref[k, 2] = jnp.concatenate([early[:, 128:], late[:, 128:]], axis=1)

    def rates(k, p):
        return [jnp.broadcast_to(rt_ref[k, i, pl.ds(p, 1), :], (8, 128)) for i in range(3)]

    def load(dat, q, t):
        lo = dat[2 * q, t]
        return [lo, lo, dat[2 * q + 1, t]]

    W_A, W_D, R_A, R_D = 0, 1, 2, 3
    zero3 = [jnp.zeros((8, 128), F32)] * 3

    def coefs(wide, slot, t, which):
        return [wide[slot, pl.ds(t * 8, 8), pl.ds((which * 3 + i) * 128, 128)] for i in range(3)]

    def held(t, slot):
        return [decays[slot, t, i] for i in range(3)], [decays[slot, t, 3 + i] for i in range(3)]

    def local_pass(p, slot, dslot, ka, kd, dat, wide, tile):
        wide[slot] = jnp.dot(tile[:, :64], pick[p], preferred_element_type=F32)
        ra, rd = rates(ka, p), rates(kd, p)

        def up(t, carry):
            fa, md = carry[:3], carry[3:]
            s = load(dat, 0, t)
            da = tri(lambda a, b: jnp.exp2(a * b), s, ra)
            dd = tri(lambda a, b: jnp.exp2(a * b), s, rd)
            for i in range(3):
                decays[dslot, t, i] = da[i]
                decays[dslot, t, 3 + i] = dd[i]
            drive = tri(mul, load(dat, 1, t), coefs(wide, slot, t, W_A))
            fa = tri(add, tri(mul, da, fa), drive)
            md = tri(mul, dd, tri(add, tri(mul, load(dat, 2, t), coefs(wide, slot, t, R_D)), md))
            return (*fa, *md)

        def down(i, carry):
            t = T - 1 - i
            ma, fd = carry[:3], carry[3:]
            da, dd = held(t, dslot)
            drive = tri(mul, load(dat, 1, t), coefs(wide, slot, t, W_D))
            fd = tri(add, tri(mul, dd, fd), drive)
            ma = tri(mul, da, tri(add, tri(mul, load(dat, 2, t), coefs(wide, slot, t, R_A)), ma))
            return (*ma, *fd)

        a = lax.fori_loop(0, T, up, (*zero3, *zero3), unroll=True)
        b = lax.fori_loop(0, T, down, (*zero3, *zero3), unroll=True)
        return a[:3], b[:3], b[3:], a[3:]

    def final_pass(p, slot, dslot, ka, kd, dat, wide, acc, zbuf, starts):
        ra, rd = rates(ka, p), rates(kd, p)
        fa0, ma0, fd0, md0 = starts

        def put(q, t, parts):
            zbuf[q, p, 0, t], zbuf[q, p, 1, t] = fold(parts, low)

        def up(t, carry):
            h, m = carry[:3], carry[3:]
            da, dd = held(t, dslot)
            sx, g = load(dat, 1, t), load(dat, 2, t)
            db = tri(mul, da, h)
            h = tri(add, db, tri(mul, sx, coefs(wide, slot, t, W_A)))
            adj = tri(add, tri(mul, g, coefs(wide, slot, t, R_D)), m)
            for i in range(3):
                keep[t, i] = db[i]
                keep[t, 3 + i] = adj[i]
            put(2, t, tri(mul, h, g))
            put(1, t, tri(mul, adj, sx))
            th = tri(mul, adj, coefs(wide, slot, t, W_D))
            keep[t, 6] = th[0] + th[1]
            keep[t, 7] = th[2]
            return (*h, *tri(mul, dd, adj))

        def down(i, carry):
            t = T - 1 - i
            m, h, acc_a, acc_d = carry[:3], carry[3:6], carry[6:9], carry[9:]
            da, dd = held(t, dslot)
            s, sx, g = load(dat, 0, t), load(dat, 1, t), load(dat, 2, t)
            db = tri(mul, dd, h)
            h = tri(add, db, tri(mul, sx, coefs(wide, slot, t, W_D)))
            adj = tri(add, tri(mul, g, coefs(wide, slot, t, R_A)), m)
            put(3, t, tri(mul, h, g))
            put(0, t, tri(mul, adj, sx))
            th = tri(mul, adj, coefs(wide, slot, t, W_A))
            acc[0, t] += keep[t, 6] + (th[0] + th[1])
            acc[1, t] += keep[t, 7] + th[2]
            mem_a = tri(mul, adj, [keep[t, i] for i in range(3)])
            mem_d = tri(mul, [keep[t, 3 + i] for i in range(3)], db)
            mr = tri(add, tri(mul, mem_a, ra), tri(mul, mem_d, rd))
            acc[2, t] += mr[0] + mr[1]
            acc[3, t] += mr[2]
            acc_a = tri(add, acc_a, tri(mul, mem_a, s))
            acc_d = tri(add, acc_d, tri(mul, mem_d, s))
            return (*tri(mul, da, adj), *h, *acc_a, *acc_d)

        lax.fori_loop(0, T, up, (*fa0, *md0), unroll=True)
        out = lax.fori_loop(0, T, down, (*ma0, *fd0, *zero3, *zero3), unroll=True)
        for k, sums in ((ka, out[6:9]), (kd, out[9:])):
            for i in range(3):
                asend[k * PAIRS + p, pl.ds(i, 1), :] = -jnp.sum(sums[i], axis=0, keepdims=True)

    def channel_sums(zbuf):
        total = None
        for q in range(4):
            whole = jnp.concatenate(
                [zbuf[q, p, j].reshape(128, 128) for p in range(PAIRS) for j in range(2)], axis=1)
            high = whole.astype(jnp.bfloat16)
            rest = (whole - high.astype(F32)).astype(jnp.bfloat16)
            part = jnp.dot(high, place[q], preferred_element_type=F32)
            part = part + jnp.dot(rest, place[q], preferred_element_type=F32)
            total = part if total is None else total + part
        return total.reshape(T, 8, 128)

    def settle(acc, t):
        th, m = acc[1, t], acc[3, t]
        return jnp.where(low, th, m) + pltpu.roll(jnp.where(low, m, th), 64, 1)

    tile_r = rowtile[...].reshape(128, 128).astype(jnp.bfloat16)
    ztile[...] = tile_r

    def row_local(p, _):
        fa, ma, fd, md = local_pass(p, p, p, 0, 1, dat_r, spread_r, ztile)
        for q, parts in enumerate((fa, ma, fd, md)):
            for i in range(3):
                csend[q * PAIRS + p, i] = parts[i]
        return 0

    lax.fori_loop(0, PAIRS, row_local, 0, unroll=2)

    def send_c(i, _):
        to = lax.rem(col + i, COLS)
        remote(csend.at[to], crecv.at[col], 2, cols=to).start()
        return 0

    lax.fori_loop(1, COLS, send_c, 0)
    crecv[col] = csend[col]

    place_k = lax.broadcasted_iota(jnp.int32, (128, 128), 0) // 64 * 8
    place_n = lax.broadcasted_iota(jnp.int32, (128, 128), 1)

    def fill_place(p, _):
        for q in range(4):
            for j, source in enumerate((place_n - place_k, place_n + place_k - 8)):
                place[q, pl.ds(pl.multiple_of(p * 256 + j * 128, 128), 128), :] = jnp.where(
                    source == 16 * q + p, 1.0, 0.0).astype(jnp.bfloat16)
        return 0

    lax.fori_loop(0, PAIRS, fill_place, 0)
    skip = jnp.zeros((1, 192), F32)
    for r in range(8):
        skip = skip + jnp.sum(g_ref[r].astype(F32) * x_ref[r].astype(F32), axis=0, keepdims=True)
    skip_lo = skip[:, :128]
    skip_hi = jnp.concatenate([skip[:, 128:], skip[:, 128:]], axis=1)
    asend[...] = jnp.zeros_like(asend)
    asend[0, 3:4, :] = skip_lo
    asend[1, 3:4, :] = skip_hi
    acc_r[...] = jnp.zeros_like(acc_r)
    acc_z[...] = jnp.zeros_like(acc_z)
    shift[...] = jnp.zeros_like(shift)

    taken(srecv.at[pl.ds(0, COLS - 1)], recv_sem, 1)
    taken(crecv.at[pl.ds(0, COLS - 1)], recv_sem, 2)
    kind = col // PAIRS
    pair = lax.rem(col, PAIRS)
    falls = jnp.where((kind == 1) | (kind == 2), 1, 0)
    own_rates = rates(kind // 2, pair)

    def chain(i, carry):
        b = i + falls * (COLS - 1 - 2 * i)
        for j in range(3):
            bsend[b, j] = carry[j]
        s_lo, s_hi = srecv[b, 0], srecv[b, 1]
        kept = tri(lambda a, r: jnp.exp2(a * r), [s_lo, s_lo, s_hi], own_rates)
        return tuple(kept[j] * carry[j] + crecv[b, j] for j in range(3))

    lax.fori_loop(0, COLS, chain, tuple(zero3), unroll=True)

    def send_b(i, _):
        to = lax.rem(col + i, COLS)
        remote(bsend.at[to], brecv.at[col], 3, cols=to).start()
        return 0

    lax.fori_loop(1, COLS, send_b, 0)
    brecv[col] = bsend[col]

    taken(zrecv.at[:, pl.ds(0, 112), :], recv_sem, 0)
    for t in range(T):
        at = pl.ds(t, 8, stride=16)
        tiles = [zrecv[q, at, :] for q in range(5)]
        unpack(dat_z, t, tiles)
        rowtile[t] = tiles[4]
    ztile[...] = rowtile[...].reshape(128, 128).astype(jnp.bfloat16)
    chunk = lax.rem(lax.broadcasted_iota(jnp.int32, (8, 128), 0), 4)
    from_chunk = {1: [chunk >= d for d in (1, 2, 3)], -1: [chunk < 4 - d for d in (1, 2, 3)]}

    def shifted(j, d):
        return shift[j, pl.ds(16 - 2 * d, 8, stride=2), :]

    def set_shift(j, value):
        shift[j, pl.ds(16, 8, stride=2), :] = value

    zs = step_sums(dat_z)
    set_shift(12, zs[0])
    set_shift(13, zs[1])
    moved = tuple(shifted(j, d) for d in (1, 2, -1, -2) for j in (12, 13))

    def line_final(p, moved):
        ends = local_pass(p, 0, PAIRS, 2, 3, dat_z, spread_z, ztile)
        for e, parts in enumerate(ends):
            for i in range(3):
                set_shift(e * 3 + i, parts[i])
        starts = []
        for e, (k, sign) in enumerate(((2, 1), (2, -1), (3, -1), (3, 1))):
            rate = rates(k, p)
            at = 0 if sign == 1 else 4
            near, far = (moved[at], moved[at], moved[at + 1]), (moved[at + 2], moved[at + 2], moved[at + 3])
            start = []
            for i in range(3):
                f1, f2, f3 = (jnp.where(from_chunk[sign][d - 1], shifted(e * 3 + i, d * sign), 0.0)
                              for d in (1, 2, 3))
                start.append(f1 + jnp.exp2(near[i] * rate[i]) * (f2 + jnp.exp2(far[i] * rate[i]) * f3))
            starts.append(start)
        final_pass(p, 0, PAIRS, 2, 3, dat_z, spread_z, acc_z, zbuf_z, starts)
        return moved

    lax.fori_loop(0, PAIRS, line_final, moved, unroll=2)
    def send_a(first):
        def one(i, _):
            to = first + lax.rem(col + i, COLS // 2)

            @pl.when(to != col)
            def _():
                remote(asend.at[to], arecv.at[col], 5, cols=to).start()
            return 0

        lax.fori_loop(0, COLS // 2, one, 0)

    send_a(COLS // 2)

    taken(brecv.at[pl.ds(0, COLS - 1)], recv_sem, 3)

    def row_final(p, _):
        starts = [[brecv[q * PAIRS + p, i] for i in range(3)] for q in range(4)]
        final_pass(p, p, p, 0, 1, dat_r, spread_r, acc_r, zbuf_r, starts)
        return 0

    lax.fori_loop(0, PAIRS, row_final, 0, unroll=2)

    send_a(0)
    arecv[col] = asend[col]

    sums = channel_sums(zbuf_z)
    for t in range(T):
        at = pl.ds(t, 8, stride=16)
        zout[0, at, :] = acc_z[0, t]
        zout[1, at, :] = acc_z[2, t]
        zout[2, at, :] = settle(acc_z, t)
        zout[3, at, :] = sums[t]

    def send_back(i, _):
        to = lax.rem(row + i, ROWS)
        for c in range(2):
            remote(zout.at[:, pl.ds(pl.multiple_of(c * 64 + to * 8, 8), 8), :],
                   zback.at[:, pl.ds(pl.multiple_of(row * 16 + c * 8, 8), 8), :], 4, rows=to).start()
        return 0

    lax.fori_loop(1, ROWS, send_back, 0)
    for c in range(2):
        zback[:, pl.ds(pl.multiple_of(row * 16 + c * 8, 8), 8), :] = (
            zout[:, pl.ds(pl.multiple_of(c * 64 + row * 8, 8), 8), :])

    taken(arecv.at[pl.ds(0, COLS - 1)], recv_sem, 5)
    zsum[row] = tree([arecv[b] for b in range(COLS)])

    def send_zsum(i, _):
        to = lax.rem(row + i, ROWS)
        remote(zsum.at[row], zsum.at[row], 6, rows=to).start()
        return 0

    lax.fori_loop(1, ROWS, send_zsum, 0)

    sums = channel_sums(zbuf_r)
    for t in range(T):
        at = pl.ds(t, 8, stride=16)
        nat[0, at, :] = acc_r[0, t]
        nat[1, at, :] = acc_r[2, t]
        nat[2, at, :] = settle(acc_r, t)
        nat[3, at, :] = sums[t]

    taken(zsum.at[pl.ds(0, ROWS - 1)], recv_sem, 6)
    fin_ref[col] = tree([zsum[b] for b in range(ROWS)])

    def send_fin(i, _):
        to = lax.rem(col + i, COLS)
        remote(fin_ref.at[col], fin_ref.at[col], 7, cols=to).start()
        return 0

    lax.fori_loop(1, COLS, send_fin, 0)

    taken(zback.at[:, pl.ds(0, 112), :], recv_sem, 4)
    for r in range(8):
        back = pl.ds(r, 16, stride=8)
        at = pl.ds(r * 16, 16)
        th_lo = nat[0, at, :] + zback[0, back, :]
        m_lo = nat[1, at, :] + zback[1, back, :]
        packed = nat[2, at, :] + zback[2, back, :]
        th_hi = packed[:, :64]
        m_hi = pltpu.roll(packed, 64, 1)[:, :64]
        xv = x_ref[r].astype(F32)
        sv = s_ref[r].astype(F32)
        gv = g_ref[r].astype(F32)
        gi_ref[r, :, :128] = sk_ref[:, :128] * gv[:, :128] + sv[:, :128] * th_lo
        gi_ref[r, :, 128:] = sk_ref[:, 128:] * gv[:, 128:] + sv[:, 128:] * th_hi
        gs_ref[r, :, :128] = th_lo * xv[:, :128] + LN2 * m_lo
        gs_ref[r, :, 128:] = th_hi * xv[:, 128:] + LN2 * m_hi
        for first, sums in ((0, nat[3, at, :]), (2, zback[3, back, :])):
            for j in range(2):
                gw_ref[first + j, r] = sums[:, 16 * j : 16 * j + 16]
                gr_ref[first + j, r] = sums[:, 32 + 16 * j : 48 + 16 * j]

    leaving = [pltpu.make_async_copy(src, dst, out_sem.at[i]) for i, (src, dst) in enumerate(
        ((gi_ref, gi_out), (gs_ref, gs_out), (gw_ref, gw_out), (gr_ref, gr_out)))]
    for copy in leaving:
        copy.start()

    taken(fin_ref.at[pl.ds(0, COLS - 1)], recv_sem, 7)
    for k in range(4):
        lo, late, hi = (jnp.concatenate([fin_ref[k * PAIRS + p, pl.ds(i, 1), :] for p in range(PAIRS)], axis=0)
                        for i in range(3))
        rate_sum[k, :8, :128] = lo
        rate_sum[k, 8:, :128] = late
        rate_sum[k, :8, 128:] = hi[:, :64]
        rate_sum[k, 8:, 128:] = hi[:, 64:]
    skip_sum[:, :128] = fin_ref[0, 3:4, :]
    skip_sum[:, 128:] = fin_ref[1, 3:4, :64]
    last = [pltpu.make_async_copy(rate_sum, rate_out, out_sem.at[4]),
            pltpu.make_async_copy(skip_sum, skip_out, out_sem.at[5])]
    for copy in last:
        copy.start()

    taken(zrecv.at[:, pl.ds(0, 112), :], send_sem, 0)
    taken(srecv.at[pl.ds(0, COLS - 1)], send_sem, 1)
    taken(crecv.at[pl.ds(0, COLS - 1)], send_sem, 2)
    taken(brecv.at[pl.ds(0, COLS - 1)], send_sem, 3)
    taken(zback.at[:, pl.ds(0, 112), :], send_sem, 4)
    taken(arecv.at[pl.ds(0, COLS - 1)], send_sem, 5)
    taken(zsum.at[pl.ds(0, ROWS - 1)], send_sem, 6)
    taken(fin_ref.at[pl.ds(0, COLS - 1)], send_sem, 7)
    for copy in leaving + last:
        copy.wait()


def leave(*refs):
    ins, outs, held, sems = refs[:6], refs[6:12], refs[12:18], refs[18]
    arrive = [pltpu.make_async_copy(ins[i], held[i], sems.at[i]) for i in range(6)]
    depart = [pltpu.make_async_copy(held[i], outs[i], sems.at[6 + i]) for i in range(6)]
    for copy in arrive:
        copy.start()
    for i in range(6):
        arrive[i].wait()
        depart[i].start()
    for copy in depart:
        copy.wait()


def on_device(inputs, step_sizes, write_coef, read_coef, rate_table, skip_gain, grad_out):
    B16 = jnp.bfloat16
    scratch = [
        pltpu.VMEM(shape, kind[0] if kind else F32)
        for shape, *kind in (
            ((8, 16, 192),),
            ((8, 16, 192),),
            ((4, 8, 16, 16),),
            ((4, 8, 16, 16),),
            ((4, 16, 192),),
            ((1, 192),),
            ((COLS, 4, 128),),
            ((8, 16, 192), B16),
            ((8, 16, 192), B16),
            ((8, 16, 192), B16),
            ((4, 8, 16, 16), B16),
            ((4, 8, 16, 16), B16),
            ((4, 16, 192),),
            ((1, 192),),
            ((4, 3, PAIRS, 128),),
            ((6, 128, 128),),
            ((5, T, 8, 128),),
            ((T, 8, 128),),
            ((6, T, 8, 128),),
            ((6, T, 8, 128),),
            ((PAIRS + 1, T, 6, 8, 128),),
            ((2, 8, 128),),
            ((COLS, 2, 8, 128),),
            ((COLS, 3, 8, 128),),
            ((COLS, 3, 8, 128),),
            ((COLS, 3, 8, 128),),
            ((COLS, 3, 8, 128),),
            ((5, 128, 128),),
            ((128, 128), B16),
            ((T, 8, 8, 128),),
            ((4, T, 8, 128),),
            ((4, T, 8, 128),),
            ((4, PAIRS, 2, T, 8, 128),),
            ((4, PAIRS, 2, T, 8, 128),),
            ((PAIRS, 64, 12 * 128), B16),
            ((4, PAIRS * 256, 128), B16),
            ((PAIRS, 128, 12 * 128),),
            ((1, 128, 12 * 128),),
            ((14, 40, 128),),
            ((4, 128, 128),),
            ((4, 128, 128),),
            ((4, 128, 128),),
            ((COLS, 4, 128),),
            ((COLS, 4, 128),),
            ((ROWS, 4, 128),),
        )
    ]
    scratch += [pltpu.SemaphoreType.DMA((8,)), pltpu.SemaphoreType.DMA((8,)), pltpu.SemaphoreType.DMA((7,)), pltpu.SemaphoreType.DMA((6,))]
    cells = jax.ShapeDtypeStruct((8, 16, 192), F32)
    kinds = jax.ShapeDtypeStruct((4, 8, 16, 16), F32)
    shapes = [cells, cells, kinds, kinds, jax.ShapeDtypeStruct((4, 16, 192), F32), jax.ShapeDtypeStruct((1, 192), F32)]
    hbm = pl.BlockSpec(memory_space=pltpu.MemorySpace.HBM)
    made = pl.pallas_call(
        body,
        out_shape=shapes,
        in_specs=[hbm] * 7,
        out_specs=[hbm] * 6,
        scratch_shapes=scratch,
        compiler_params=pltpu.CompilerParams(
            collective_id=0, has_side_effects=True, vmem_limit_bytes=60 * 1024 * 1024),
    )(inputs, step_sizes, grad_out, write_coef, read_coef, rate_table.transpose(0, 2, 1), skip_gain.reshape(1, 192))
    gi, gs, gw, gr, rate, skip = pl.pallas_call(
        leave,
        out_shape=shapes,
        in_specs=[hbm] * 6,
        out_specs=[hbm] * 6,
        scratch_shapes=[pltpu.VMEM(a.shape, F32) for a in shapes] + [pltpu.SemaphoreType.DMA((12,))],
        compiler_params=pltpu.CompilerParams(vmem_limit_bytes=60 * 1024 * 1024),
    )(*made)
    return gi, gs, gw, gr, rate.transpose(0, 2, 1), skip.reshape(192)


def solution(mesh):
    cells, coefs = P("rows", "cols", None), P(None, "rows", "cols", None)
    return jax.shard_map(
        on_device, mesh=mesh, in_specs=(cells, cells, coefs, coefs, P(), P(), cells),
        out_specs=(cells, cells, coefs, coefs, P(), P()), check_vma=False)
```

```python
import functools
import math

import jax
import jax.numpy as jnp
from jax import lax
from jax.experimental import pallas as pl
from jax.experimental.pallas import tpu as pltpu
from jax.sharding import PartitionSpec as P

F32 = jnp.float32
T = 16
PAIRS = 8
LOG2E = 1.4426950408889634
LN2 = 0.6931471805599453
COLS = 32
ROWS = 8


def low_half():
    return lax.broadcasted_iota(jnp.int32, (8, 128), 1) < 64


def fold(q, low):
    return jnp.where(low, q[0], q[1]) + q[2], jnp.where(low, q[1], q[0])


def tri(f, *groups):
    return [f(*parts) for parts in zip(*groups)]


def ring(d, n):
    return min(d, n - d)


HOPS = sorted(((dx, dy, dc) for dx in range(4) for dy in range(4) for dc in range(2) if dx or dy or dc),
              key=lambda d: -(ring(d[0], 4) + ring(d[1], 4)))
ROW_HOPS = sorted(range(1, ROWS), key=lambda d: -ring(d, ROWS))


def tree(parts):
    while len(parts) > 1:
        parts = [a + b for a, b in zip(parts[::2], parts[1::2])]
    return parts[0]


def add(a, b):
    return a + b


def mul(a, b):
    return a * b


def body(x_in, s_in, g_in, w_in, r_in, rate_in, sk_in,
         gi_out, gs_out, gw_out, gr_out, rate_out, skip_out,
         gi_ref, gs_ref, gw_ref, gr_ref, rate_sum, skip_sum, fin_ref,
         x_ref, s_ref, g_ref, w_ref, r_ref, rate_ref, sk_ref, rt_ref,
         flat, zmsg, rowtile, dat_r, dat_z, decays, ssend, srecv, csend, crecv, bsend, brecv,
         zrecv, ztile, keep, acc_r, acc_z, zbuf_r, zbuf_z, pick, place, spread_r, spread_z, shift, nat,
         zout, zback, asend, arecv, zsum, send_sem, recv_sem, in_sem, out_sem):
    entries = [pltpu.make_async_copy(src, dst, in_sem.at[i]) for i, (src, dst) in enumerate(
        ((x_in, x_ref), (s_in, s_ref), (g_in, g_ref), (w_in, w_ref), (r_in, r_ref), (rate_in, rate_ref), (sk_in, sk_ref)))]
    for entry in entries:
        entry.start()
    col = lax.axis_index("cols")
    row = lax.axis_index("rows")
    low = low_half()

    def col_at(d):
        return (lax.rem(col // 8 + d[0], 4) * 8 + lax.rem(lax.rem(col // 2, 4) + d[1], 4) * 2
                + lax.rem(lax.rem(col, 2) + d[2], 2))

    barrier = pltpu.get_barrier_semaphore()

    def greet_cols(i, _):
        pl.semaphore_signal(barrier, inc=1, device_id={"cols": lax.rem(col + i, COLS)},
                            device_id_type=pl.DeviceIdType.MESH)
        return 0

    def greet_rows(i, _):
        pl.semaphore_signal(barrier, inc=1, device_id={"rows": lax.rem(row + i, ROWS)},
                            device_id_type=pl.DeviceIdType.MESH)
        return 0

    lax.fori_loop(1, COLS, greet_cols, 0)
    lax.fori_loop(1, ROWS, greet_rows, 0)

    def remote(src, dst, n, **to):
        return pltpu.make_async_remote_copy(
            src_ref=src, dst_ref=dst, send_sem=send_sem.at[n], recv_sem=recv_sem.at[n],
            device_id=to, device_id_type=pl.DeviceIdType.MESH)

    def taken(ref, sem, n):
        pltpu.make_async_copy(ref, ref, sem.at[n]).wait()

    for entry in entries:
        entry.wait()
    for r in range(8):
        sv = s_ref[r].astype(F32)
        gv = g_ref[r].astype(F32)
        pv = sv * x_ref[r].astype(F32)
        at = pl.ds(r * 16, 16)
        flat[0, at, :] = sv[:, :128]
        flat[1, at, :] = pv[:, :128]
        flat[2, at, :] = gv[:, :128]
        flat[3, at, :] = jnp.concatenate([sv[:, 128:], pv[:, 128:]], axis=1)

    def to_lanes(width, start):
        r = lax.broadcasted_iota(jnp.int32, (width, 128), 0)
        c = lax.broadcasted_iota(jnp.int32, (width, 128), 1)
        return jnp.where(c == r + start, 1.0, 0.0).astype(jnp.bfloat16)

    upper = jnp.dot(g_ref[:, :, 128:].reshape(128, 64), to_lanes(64, 64), preferred_element_type=F32)
    for q, first in ((4, 2), (5, 0)):
        tile = upper
        for which, (ref, k) in enumerate((ref, first + j) for ref in (w_ref, r_ref) for j in range(2)):
            tile = tile + jnp.dot(ref[k].reshape(128, 16), to_lanes(16, 16 * which), preferred_element_type=F32)
        flat[q] = tile

    for t in range(T):
        at = pl.ds(t, 8, stride=16)
        for q in range(5):
            zmsg[q, t] = flat[q, at, :]
        rowtile[t] = flat[5, at, :]

    def unpack(dat, t, tiles):
        s_lo, p_lo, g_lo, sp, gc = tiles
        spr = pltpu.roll(sp, 64, 1)
        dat[0, t] = s_lo
        dat[1, t] = jnp.where(low, sp, spr)
        dat[2, t] = p_lo
        dat[3, t] = jnp.where(low, spr, sp)
        dat[4, t] = g_lo
        dat[5, t] = jnp.where(low, pltpu.roll(gc, 64, 1), gc)

    def step_sums(dat):
        lo, hi = dat[0, 0], dat[1, 0]
        for t in range(1, T):
            lo, hi = lo + dat[0, t], hi + dat[1, t]
        return lo, hi

    pl.semaphore_wait(barrier, COLS - 1 + ROWS - 1)

    for d in ROW_HOPS:
        to = lax.rem(row + d, ROWS)
        for c in range(2):
            remote(zmsg.at[:, 2 * to + c],
                   zrecv.at[:, pl.ds(pl.multiple_of(c * 64 + row * 8, 8), 8), :], 0, rows=to).start()
    for c in range(2):
        for q in range(5):
            zrecv[q, pl.ds(pl.multiple_of(c * 64 + row * 8, 8), 8), :] = zmsg[q, 2 * row + c]

    s_lo, sp = zmsg[0, 0], zmsg[3, 0]
    for t in range(1, T):
        s_lo, sp = s_lo + zmsg[0, t], sp + zmsg[3, t]
    ssend[0] = s_lo
    ssend[1] = jnp.where(low, sp, pltpu.roll(sp, 64, 1))
    srecv[col] = ssend[...]

    for d in HOPS:
        to = col_at(d)
        remote(ssend, srecv.at[col], 1, cols=to).start()
    for t in range(T):
        unpack(dat_r, t, (zmsg[0, t], zmsg[1, t], zmsg[2, t], zmsg[3, t], rowtile[t]))

    pick_j = lax.broadcasted_iota(jnp.int32, (64, 128), 0)
    pick_up = pick_j - jnp.where(lax.broadcasted_iota(jnp.int32, (64, 128), 1) < 64, 0, 8)

    def fill_pick(p, _):
        for which in range(4):
            base = 16 * which
            for i, (source, start) in enumerate(((pick_j, base), (pick_j, base + 8), (pick_up, base))):
                pick[p, :, pl.ds((which * 3 + i) * 128, 128)] = jnp.where(
                    source == start + p, 1.0, 0.0).astype(jnp.bfloat16)
        return 0

    lax.fori_loop(0, PAIRS, fill_pick, 0)

    for k in range(4):
        early, late = rate_ref[k, :8] * -LOG2E, rate_ref[k, 8:] * -LOG2E
        rt_ref[k, 0] = early[:, :128]
        rt_ref[k, 1] = late[:, :128]
        rt_ref[k, 2] = jnp.concatenate([early[:, 128:], late[:, 128:]], axis=1)

    def rates(k, p):
        return [jnp.broadcast_to(rt_ref[k, i, pl.ds(p, 1), :], (8, 128)) for i in range(3)]

    def load(dat, q, t):
        lo = dat[2 * q, t]
        return [lo, lo, dat[2 * q + 1, t]]

    W_A, W_D, R_A, R_D = 0, 1, 2, 3
    zero3 = [jnp.zeros((8, 128), F32)] * 3

    def coefs(wide, slot, t, which):
        return [wide[slot, pl.ds(t * 8, 8), pl.ds((which * 3 + i) * 128, 128)] for i in range(3)]

    def held(t, slot):
        return [decays[slot, t, i] for i in range(3)], [decays[slot, t, 3 + i] for i in range(3)]

    def local_pass(p, slot, dslot, ka, kd, dat, wide, tile):
        wide[slot] = jnp.dot(tile[:, :64], pick[p], preferred_element_type=F32)
        ra, rd = rates(ka, p), rates(kd, p)

        def up(t, carry):
            fa, md = carry[:3], carry[3:]
            s = load(dat, 0, t)
            da = tri(lambda a, b: jnp.exp2(a * b), s, ra)
            dd = tri(lambda a, b: jnp.exp2(a * b), s, rd)
            for i in range(3):
                decays[dslot, t, i] = da[i]
                decays[dslot, t, 3 + i] = dd[i]
            drive = tri(mul, load(dat, 1, t), coefs(wide, slot, t, W_A))
            fa = tri(add, tri(mul, da, fa), drive)
            md = tri(mul, dd, tri(add, tri(mul, load(dat, 2, t), coefs(wide, slot, t, R_D)), md))
            return (*fa, *md)

        def down(i, carry):
            t = T - 1 - i
            ma, fd = carry[:3], carry[3:]
            da, dd = held(t, dslot)
            drive = tri(mul, load(dat, 1, t), coefs(wide, slot, t, W_D))
            fd = tri(add, tri(mul, dd, fd), drive)
            ma = tri(mul, da, tri(add, tri(mul, load(dat, 2, t), coefs(wide, slot, t, R_A)), ma))
            return (*ma, *fd)

        a = lax.fori_loop(0, T, up, (*zero3, *zero3), unroll=True)
        b = lax.fori_loop(0, T, down, (*zero3, *zero3), unroll=True)
        return a[:3], b[:3], b[3:], a[3:]

    def final_pass(p, slot, dslot, ka, kd, dat, wide, acc, zbuf, starts):
        ra, rd = rates(ka, p), rates(kd, p)
        fa0, ma0, fd0, md0 = starts

        def put(q, t, parts):
            zbuf[q, p, 0, t], zbuf[q, p, 1, t] = fold(parts, low)

        def up(t, carry):
            h, m = carry[:3], carry[3:]
            da, dd = held(t, dslot)
            sx, g = load(dat, 1, t), load(dat, 2, t)
            db = tri(mul, da, h)
            h = tri(add, db, tri(mul, sx, coefs(wide, slot, t, W_A)))
            adj = tri(add, tri(mul, g, coefs(wide, slot, t, R_D)), m)
            for i in range(3):
                keep[t, i] = db[i]
                keep[t, 3 + i] = adj[i]
            put(2, t, tri(mul, h, g))
            put(1, t, tri(mul, adj, sx))
            th = tri(mul, adj, coefs(wide, slot, t, W_D))
            keep[t, 6] = th[0] + th[1]
            keep[t, 7] = th[2]
            return (*h, *tri(mul, dd, adj))

        def down(i, carry):
            t = T - 1 - i
            m, h, acc_a, acc_d = carry[:3], carry[3:6], carry[6:9], carry[9:]
            da, dd = held(t, dslot)
            s, sx, g = load(dat, 0, t), load(dat, 1, t), load(dat, 2, t)
            db = tri(mul, dd, h)
            h = tri(add, db, tri(mul, sx, coefs(wide, slot, t, W_D)))
            adj = tri(add, tri(mul, g, coefs(wide, slot, t, R_A)), m)
            put(3, t, tri(mul, h, g))
            put(0, t, tri(mul, adj, sx))
            th = tri(mul, adj, coefs(wide, slot, t, W_A))
            acc[0, t] += keep[t, 6] + (th[0] + th[1])
            acc[1, t] += keep[t, 7] + th[2]
            mem_a = tri(mul, adj, [keep[t, i] for i in range(3)])
            mem_d = tri(mul, [keep[t, 3 + i] for i in range(3)], db)
            mr = tri(add, tri(mul, mem_a, ra), tri(mul, mem_d, rd))
            acc[2, t] += mr[0] + mr[1]
            acc[3, t] += mr[2]
            acc_a = tri(add, acc_a, tri(mul, mem_a, s))
            acc_d = tri(add, acc_d, tri(mul, mem_d, s))
            return (*tri(mul, da, adj), *h, *acc_a, *acc_d)

        lax.fori_loop(0, T, up, (*fa0, *md0), unroll=True)
        out = lax.fori_loop(0, T, down, (*ma0, *fd0, *zero3, *zero3), unroll=True)
        for k, sums in ((ka, out[6:9]), (kd, out[9:])):
            for i in range(3):
                asend[k * PAIRS + p, pl.ds(i, 1), :] = -jnp.sum(sums[i], axis=0, keepdims=True)

    def channel_sums(zbuf):
        total = None
        for q in range(4):
            whole = jnp.concatenate(
                [zbuf[q, p, j].reshape(128, 128) for p in range(PAIRS) for j in range(2)], axis=1)
            high = whole.astype(jnp.bfloat16)
            rest = (whole - high.astype(F32)).astype(jnp.bfloat16)
            part = jnp.dot(high, place[q], preferred_element_type=F32)
            part = part + jnp.dot(rest, place[q], preferred_element_type=F32)
            total = part if total is None else total + part
        return total.reshape(T, 8, 128)

    def settle(acc, t):
        th, m = acc[1, t], acc[3, t]
        return jnp.where(low, th, m) + pltpu.roll(jnp.where(low, m, th), 64, 1)

    tile_r = rowtile[...].reshape(128, 128).astype(jnp.bfloat16)
    ztile[...] = tile_r

    def row_local(p, _):
        fa, ma, fd, md = local_pass(p, p, p, 0, 1, dat_r, spread_r, ztile)
        for q, parts in enumerate((fa, ma, fd, md)):
            for i in range(3):
                csend[q * PAIRS + p, i] = parts[i]
        return 0

    lax.fori_loop(0, PAIRS, row_local, 0, unroll=2)

    for d in HOPS:
        to = col_at(d)
        remote(csend.at[to], crecv.at[col], 2, cols=to).start()
    crecv[col] = csend[col]

    place_k = lax.broadcasted_iota(jnp.int32, (128, 128), 0) // 64 * 8
    place_n = lax.broadcasted_iota(jnp.int32, (128, 128), 1)

    def fill_place(p, _):
        for q in range(4):
            for j, source in enumerate((place_n - place_k, place_n + place_k - 8)):
                place[q, pl.ds(pl.multiple_of(p * 256 + j * 128, 128), 128), :] = jnp.where(
                    source == 16 * q + p, 1.0, 0.0).astype(jnp.bfloat16)
        return 0

    lax.fori_loop(0, PAIRS, fill_place, 0)
    skip = jnp.zeros((1, 192), F32)
    for r in range(8):
        skip = skip + jnp.sum(g_ref[r].astype(F32) * x_ref[r].astype(F32), axis=0, keepdims=True)
    skip_lo = skip[:, :128]
    skip_hi = jnp.concatenate([skip[:, 128:], skip[:, 128:]], axis=1)
    asend[...] = jnp.zeros_like(asend)
    asend[0, 3:4, :] = skip_lo
    asend[1, 3:4, :] = skip_hi
    acc_r[...] = jnp.zeros_like(acc_r)
    acc_z[...] = jnp.zeros_like(acc_z)
    shift[...] = jnp.zeros_like(shift)

    taken(srecv.at[pl.ds(0, COLS - 1)], recv_sem, 1)
    taken(crecv.at[pl.ds(0, COLS - 1)], recv_sem, 2)
    kind = col // PAIRS
    pair = lax.rem(col, PAIRS)
    falls = jnp.where((kind == 1) | (kind == 2), 1, 0)
    own_rates = rates(kind // 2, pair)

    def chain(i, carry):
        b = i + falls * (COLS - 1 - 2 * i)
        for j in range(3):
            bsend[b, j] = carry[j]
        s_lo, s_hi = srecv[b, 0], srecv[b, 1]
        kept = tri(lambda a, r: jnp.exp2(a * r), [s_lo, s_lo, s_hi], own_rates)
        return tuple(kept[j] * carry[j] + crecv[b, j] for j in range(3))

    lax.fori_loop(0, COLS, chain, tuple(zero3), unroll=True)

    for d in HOPS:
        to = col_at(d)
        remote(bsend.at[to], brecv.at[col], 3, cols=to).start()
    brecv[col] = bsend[col]

    taken(zrecv.at[:, pl.ds(0, 112), :], recv_sem, 0)
    for t in range(T):
        at = pl.ds(t, 8, stride=16)
        tiles = [zrecv[q, at, :] for q in range(5)]
        unpack(dat_z, t, tiles)
        rowtile[t] = tiles[4]
    ztile[...] = rowtile[...].reshape(128, 128).astype(jnp.bfloat16)
    chunk = lax.rem(lax.broadcasted_iota(jnp.int32, (8, 128), 0), 4)
    from_chunk = {1: [chunk >= d for d in (1, 2, 3)], -1: [chunk < 4 - d for d in (1, 2, 3)]}

    def shifted(j, d):
        return shift[j, pl.ds(16 - 2 * d, 8, stride=2), :]

    def set_shift(j, value):
        shift[j, pl.ds(16, 8, stride=2), :] = value

    zs = step_sums(dat_z)
    set_shift(12, zs[0])
    set_shift(13, zs[1])
    moved = tuple(shifted(j, d) for d in (1, 2, -1, -2) for j in (12, 13))

    def line_final(p, moved):
        ends = local_pass(p, 0, PAIRS, 2, 3, dat_z, spread_z, ztile)
        for e, parts in enumerate(ends):
            for i in range(3):
                set_shift(e * 3 + i, parts[i])
        starts = []
        for e, (k, sign) in enumerate(((2, 1), (2, -1), (3, -1), (3, 1))):
            rate = rates(k, p)
            at = 0 if sign == 1 else 4
            near, far = (moved[at], moved[at], moved[at + 1]), (moved[at + 2], moved[at + 2], moved[at + 3])
            start = []
            for i in range(3):
                f1, f2, f3 = (jnp.where(from_chunk[sign][d - 1], shifted(e * 3 + i, d * sign), 0.0)
                              for d in (1, 2, 3))
                start.append(f1 + jnp.exp2(near[i] * rate[i]) * (f2 + jnp.exp2(far[i] * rate[i]) * f3))
            starts.append(start)
        final_pass(p, 0, PAIRS, 2, 3, dat_z, spread_z, acc_z, zbuf_z, starts)
        return moved

    lax.fori_loop(0, PAIRS, line_final, moved, unroll=2)
    def send_a(first):
        def one(i, _):
            to = first + lax.rem(col + i, COLS // 2)

            @pl.when(to != col)
            def _():
                remote(asend.at[to], arecv.at[col], 5, cols=to).start()
            return 0

        lax.fori_loop(0, COLS // 2, one, 0)

    send_a(COLS // 2)

    taken(brecv.at[pl.ds(0, COLS - 1)], recv_sem, 3)

    def row_final(p, _):
        starts = [[brecv[q * PAIRS + p, i] for i in range(3)] for q in range(4)]
        final_pass(p, p, p, 0, 1, dat_r, spread_r, acc_r, zbuf_r, starts)
        return 0

    lax.fori_loop(0, PAIRS, row_final, 0, unroll=2)

    send_a(0)
    arecv[col] = asend[col]

    sums = channel_sums(zbuf_z)
    for t in range(T):
        at = pl.ds(t, 8, stride=16)
        zout[0, at, :] = acc_z[0, t]
        zout[1, at, :] = acc_z[2, t]
        zout[2, at, :] = settle(acc_z, t)
        zout[3, at, :] = sums[t]

    for d in ROW_HOPS:
        to = lax.rem(row + d, ROWS)
        for c in range(2):
            remote(zout.at[:, pl.ds(pl.multiple_of(c * 64 + to * 8, 8), 8), :],
                   zback.at[:, pl.ds(pl.multiple_of(row * 16 + c * 8, 8), 8), :], 4, rows=to).start()
    for c in range(2):
        zback[:, pl.ds(pl.multiple_of(row * 16 + c * 8, 8), 8), :] = (
            zout[:, pl.ds(pl.multiple_of(c * 64 + row * 8, 8), 8), :])

    taken(arecv.at[pl.ds(0, COLS - 1)], recv_sem, 5)
    zsum[row] = tree([arecv[b] for b in range(COLS)])

    def send_zsum(i, _):
        to = lax.rem(row + i, ROWS)
        remote(zsum.at[row], zsum.at[row], 6, rows=to).start()
        return 0

    lax.fori_loop(1, ROWS, send_zsum, 0)

    sums = channel_sums(zbuf_r)
    for t in range(T):
        at = pl.ds(t, 8, stride=16)
        nat[0, at, :] = acc_r[0, t]
        nat[1, at, :] = acc_r[2, t]
        nat[2, at, :] = settle(acc_r, t)
        nat[3, at, :] = sums[t]

    taken(zsum.at[pl.ds(0, ROWS - 1)], recv_sem, 6)
    fin_ref[col] = tree([zsum[b] for b in range(ROWS)])

    def send_fin(i, _):
        to = lax.rem(col + i, COLS)
        remote(fin_ref.at[col], fin_ref.at[col], 7, cols=to).start()
        return 0

    lax.fori_loop(1, COLS, send_fin, 0)

    taken(zback.at[:, pl.ds(0, 112), :], recv_sem, 4)
    for r in range(8):
        back = pl.ds(r, 16, stride=8)
        at = pl.ds(r * 16, 16)
        th_lo = nat[0, at, :] + zback[0, back, :]
        m_lo = nat[1, at, :] + zback[1, back, :]
        packed = nat[2, at, :] + zback[2, back, :]
        th_hi = packed[:, :64]
        m_hi = pltpu.roll(packed, 64, 1)[:, :64]
        xv = x_ref[r].astype(F32)
        sv = s_ref[r].astype(F32)
        gv = g_ref[r].astype(F32)
        gi_ref[r, :, :128] = sk_ref[:, :128] * gv[:, :128] + sv[:, :128] * th_lo
        gi_ref[r, :, 128:] = sk_ref[:, 128:] * gv[:, 128:] + sv[:, 128:] * th_hi
        gs_ref[r, :, :128] = th_lo * xv[:, :128] + LN2 * m_lo
        gs_ref[r, :, 128:] = th_hi * xv[:, 128:] + LN2 * m_hi
        for first, sums in ((0, nat[3, at, :]), (2, zback[3, back, :])):
            for j in range(2):
                gw_ref[first + j, r] = sums[:, 16 * j : 16 * j + 16]
                gr_ref[first + j, r] = sums[:, 32 + 16 * j : 48 + 16 * j]

    leaving = [pltpu.make_async_copy(src, dst, out_sem.at[i]) for i, (src, dst) in enumerate(
        ((gi_ref, gi_out), (gs_ref, gs_out), (gw_ref, gw_out), (gr_ref, gr_out)))]
    for copy in leaving:
        copy.start()

    taken(fin_ref.at[pl.ds(0, COLS - 1)], recv_sem, 7)
    for k in range(4):
        lo, late, hi = (jnp.concatenate([fin_ref[k * PAIRS + p, pl.ds(i, 1), :] for p in range(PAIRS)], axis=0)
                        for i in range(3))
        rate_sum[k, :8, :128] = lo
        rate_sum[k, 8:, :128] = late
        rate_sum[k, :8, 128:] = hi[:, :64]
        rate_sum[k, 8:, 128:] = hi[:, 64:]
    skip_sum[:, :128] = fin_ref[0, 3:4, :]
    skip_sum[:, 128:] = fin_ref[1, 3:4, :64]
    last = [pltpu.make_async_copy(rate_sum, rate_out, out_sem.at[4]),
            pltpu.make_async_copy(skip_sum, skip_out, out_sem.at[5])]
    for copy in last:
        copy.start()

    taken(zrecv.at[:, pl.ds(0, 112), :], send_sem, 0)
    taken(srecv.at[pl.ds(0, COLS - 1)], send_sem, 1)
    taken(crecv.at[pl.ds(0, COLS - 1)], send_sem, 2)
    taken(brecv.at[pl.ds(0, COLS - 1)], send_sem, 3)
    taken(zback.at[:, pl.ds(0, 112), :], send_sem, 4)
    taken(arecv.at[pl.ds(0, COLS - 1)], send_sem, 5)
    taken(zsum.at[pl.ds(0, ROWS - 1)], send_sem, 6)
    taken(fin_ref.at[pl.ds(0, COLS - 1)], send_sem, 7)
    for copy in leaving + last:
        copy.wait()


def leave(*refs):
    ins, outs, held, sems = refs[:6], refs[6:12], refs[12:18], refs[18]
    arrive = [pltpu.make_async_copy(ins[i], held[i], sems.at[i]) for i in range(6)]
    depart = [pltpu.make_async_copy(held[i], outs[i], sems.at[6 + i]) for i in range(6)]
    for copy in arrive:
        copy.start()
    for i in range(6):
        arrive[i].wait()
        depart[i].start()
    for copy in depart:
        copy.wait()


def on_device(inputs, step_sizes, write_coef, read_coef, rate_table, skip_gain, grad_out):
    B16 = jnp.bfloat16
    scratch = [
        pltpu.VMEM(shape, kind[0] if kind else F32)
        for shape, *kind in (
            ((8, 16, 192),),
            ((8, 16, 192),),
            ((4, 8, 16, 16),),
            ((4, 8, 16, 16),),
            ((4, 16, 192),),
            ((1, 192),),
            ((COLS, 4, 128),),
            ((8, 16, 192), B16),
            ((8, 16, 192), B16),
            ((8, 16, 192), B16),
            ((4, 8, 16, 16), B16),
            ((4, 8, 16, 16), B16),
            ((4, 16, 192),),
            ((1, 192),),
            ((4, 3, PAIRS, 128),),
            ((6, 128, 128),),
            ((5, T, 8, 128),),
            ((T, 8, 128),),
            ((6, T, 8, 128),),
            ((6, T, 8, 128),),
            ((PAIRS + 1, T, 6, 8, 128),),
            ((2, 8, 128),),
            ((COLS, 2, 8, 128),),
            ((COLS, 3, 8, 128),),
            ((COLS, 3, 8, 128),),
            ((COLS, 3, 8, 128),),
            ((COLS, 3, 8, 128),),
            ((5, 128, 128),),
            ((128, 128), B16),
            ((T, 8, 8, 128),),
            ((4, T, 8, 128),),
            ((4, T, 8, 128),),
            ((4, PAIRS, 2, T, 8, 128),),
            ((4, PAIRS, 2, T, 8, 128),),
            ((PAIRS, 64, 12 * 128), B16),
            ((4, PAIRS * 256, 128), B16),
            ((PAIRS, 128, 12 * 128),),
            ((1, 128, 12 * 128),),
            ((14, 40, 128),),
            ((4, 128, 128),),
            ((4, 128, 128),),
            ((4, 128, 128),),
            ((COLS, 4, 128),),
            ((COLS, 4, 128),),
            ((ROWS, 4, 128),),
        )
    ]
    scratch += [pltpu.SemaphoreType.DMA((8,)), pltpu.SemaphoreType.DMA((8,)), pltpu.SemaphoreType.DMA((7,)), pltpu.SemaphoreType.DMA((6,))]
    cells = jax.ShapeDtypeStruct((8, 16, 192), F32)
    kinds = jax.ShapeDtypeStruct((4, 8, 16, 16), F32)
    shapes = [cells, cells, kinds, kinds, jax.ShapeDtypeStruct((4, 16, 192), F32), jax.ShapeDtypeStruct((1, 192), F32)]
    hbm = pl.BlockSpec(memory_space=pltpu.MemorySpace.HBM)
    made = pl.pallas_call(
        body,
        out_shape=shapes,
        in_specs=[hbm] * 7,
        out_specs=[hbm] * 6,
        scratch_shapes=scratch,
        compiler_params=pltpu.CompilerParams(
            collective_id=0, has_side_effects=True, vmem_limit_bytes=60 * 1024 * 1024),
    )(inputs, step_sizes, grad_out, write_coef, read_coef, rate_table.transpose(0, 2, 1), skip_gain.reshape(1, 192))
    gi, gs, gw, gr, rate, skip = pl.pallas_call(
        leave,
        out_shape=shapes,
        in_specs=[hbm] * 6,
        out_specs=[hbm] * 6,
        scratch_shapes=[pltpu.VMEM(a.shape, F32) for a in shapes] + [pltpu.SemaphoreType.DMA((12,))],
        compiler_params=pltpu.CompilerParams(vmem_limit_bytes=60 * 1024 * 1024),
    )(*made)
    return gi, gs, gw, gr, rate.transpose(0, 2, 1), skip.reshape(192)


def solution(mesh):
    cells, coefs = P("rows", "cols", None), P(None, "rows", "cols", None)
    return jax.shard_map(
        on_device, mesh=mesh, in_specs=(cells, cells, coefs, coefs, P(), P(), cells),
        out_specs=(cells, cells, coefs, coefs, P(), P()), check_vma=False)
```

```python
import functools
import math

import jax
import jax.numpy as jnp
from jax import lax
from jax.experimental import pallas as pl
from jax.experimental.pallas import tpu as pltpu
from jax.sharding import PartitionSpec as P

F32 = jnp.float32
T = 16
PAIRS = 8
LOG2E = 1.4426950408889634
LN2 = 0.6931471805599453
COLS = 32
ROWS = 8


def low_half():
    return lax.broadcasted_iota(jnp.int32, (8, 128), 1) < 64


def fold(q, low):
    return jnp.where(low, q[0], q[1]) + q[2], jnp.where(low, q[1], q[0])


def tri(f, *groups):
    return [f(*parts) for parts in zip(*groups)]


def ring(d, n):
    return min(d, n - d)


HOPS = sorted(((dx, dy, dc) for dx in range(4) for dy in range(4) for dc in range(2) if dx or dy or dc),
              key=lambda d: -(ring(d[0], 4) + ring(d[1], 4)))
ROW_HOPS = sorted(range(1, ROWS), key=lambda d: -ring(d, ROWS))


def tree(parts):
    while len(parts) > 1:
        parts = [a + b for a, b in zip(parts[::2], parts[1::2])]
    return parts[0]


def add(a, b):
    return a + b


def mul(a, b):
    return a * b


def body(x_in, s_in, g_in, w_in, r_in, rate_in, sk_in,
         gi_out, gs_out, gw_out, gr_out, rate_out, skip_out,
         gi_ref, gs_ref, gw_ref, gr_ref, rate_sum, skip_sum, fin_ref,
         x_ref, s_ref, g_ref, w_ref, r_ref, rate_ref, sk_ref, rt_ref,
         flat, zmsg, rowtile, dat_r, dat_z, decays, ssend, srecv, csend, crecv, bsend, brecv,
         zrecv, ztile, keep, acc_r, acc_z, zbuf_r, zbuf_z, pick, place, spread_r, spread_z, shift, nat,
         zout, zback, asend, arecv, zsum, send_sem, recv_sem, in_sem, out_sem):
    entries = [pltpu.make_async_copy(src, dst, in_sem.at[i]) for i, (src, dst) in enumerate(
        ((x_in, x_ref), (s_in, s_ref), (g_in, g_ref), (w_in, w_ref), (r_in, r_ref), (rate_in, rate_ref), (sk_in, sk_ref)))]
    for entry in entries:
        entry.start()
    col = lax.axis_index("cols")
    row = lax.axis_index("rows")
    low = low_half()

    def col_at(d):
        return (lax.rem(col // 8 + d[0], 4) * 8 + lax.rem(lax.rem(col // 2, 4) + d[1], 4) * 2
                + lax.rem(lax.rem(col, 2) + d[2], 2))

    barrier = pltpu.get_barrier_semaphore()

    def greet_cols(i, _):
        pl.semaphore_signal(barrier, inc=1, device_id={"cols": lax.rem(col + i, COLS)},
                            device_id_type=pl.DeviceIdType.MESH)
        return 0

    def greet_rows(i, _):
        pl.semaphore_signal(barrier, inc=1, device_id={"rows": lax.rem(row + i, ROWS)},
                            device_id_type=pl.DeviceIdType.MESH)
        return 0

    lax.fori_loop(1, COLS, greet_cols, 0)
    lax.fori_loop(1, ROWS, greet_rows, 0)

    def remote(src, dst, n, **to):
        return pltpu.make_async_remote_copy(
            src_ref=src, dst_ref=dst, send_sem=send_sem.at[n], recv_sem=recv_sem.at[n],
            device_id=to, device_id_type=pl.DeviceIdType.MESH)

    def taken(ref, sem, n):
        pltpu.make_async_copy(ref, ref, sem.at[n]).wait()

    for entry in entries:
        entry.wait()
    for r in range(8):
        sv = s_ref[r].astype(F32)
        gv = g_ref[r].astype(F32)
        pv = sv * x_ref[r].astype(F32)
        at = pl.ds(r * 16, 16)
        flat[0, at, :] = sv[:, :128]
        flat[1, at, :] = pv[:, :128]
        flat[2, at, :] = gv[:, :128]
        flat[3, at, :] = jnp.concatenate([sv[:, 128:], pv[:, 128:]], axis=1)

    def to_lanes(width, start):
        r = lax.broadcasted_iota(jnp.int32, (width, 128), 0)
        c = lax.broadcasted_iota(jnp.int32, (width, 128), 1)
        return jnp.where(c == r + start, 1.0, 0.0).astype(jnp.bfloat16)

    upper = jnp.dot(g_ref[:, :, 128:].reshape(128, 64), to_lanes(64, 64), preferred_element_type=F32)
    for q, first in ((4, 2), (5, 0)):
        tile = upper
        for which, (ref, k) in enumerate((ref, first + j) for ref in (w_ref, r_ref) for j in range(2)):
            tile = tile + jnp.dot(ref[k].reshape(128, 16), to_lanes(16, 16 * which), preferred_element_type=F32)
        flat[q] = tile

    for t in range(T):
        at = pl.ds(t, 8, stride=16)
        for q in range(5):
            zmsg[q, t] = flat[q, at, :]
        rowtile[t] = flat[5, at, :]

    def unpack(dat, t, tiles):
        s_lo, p_lo, g_lo, sp, gc = tiles
        spr = pltpu.roll(sp, 64, 1)
        dat[0, t] = s_lo
        dat[1, t] = jnp.where(low, sp, spr)
        dat[2, t] = p_lo
        dat[3, t] = jnp.where(low, spr, sp)
        dat[4, t] = g_lo
        dat[5, t] = jnp.where(low, pltpu.roll(gc, 64, 1), gc)

    def step_sums(dat):
        lo, hi = dat[0, 0], dat[1, 0]
        for t in range(1, T):
            lo, hi = lo + dat[0, t], hi + dat[1, t]
        return lo, hi

    pl.semaphore_wait(barrier, COLS - 1 + ROWS - 1)

    for d in ROW_HOPS:
        to = lax.rem(row + d, ROWS)
        for c in range(2):
            remote(zmsg.at[:, 2 * to + c],
                   zrecv.at[:, pl.ds(pl.multiple_of(c * 64 + row * 8, 8), 8), :], 0, rows=to).start()
    for c in range(2):
        for q in range(5):
            zrecv[q, pl.ds(pl.multiple_of(c * 64 + row * 8, 8), 8), :] = zmsg[q, 2 * row + c]

    s_lo, sp = zmsg[0, 0], zmsg[3, 0]
    for t in range(1, T):
        s_lo, sp = s_lo + zmsg[0, t], sp + zmsg[3, t]
    ssend[0] = s_lo
    ssend[1] = jnp.where(low, sp, pltpu.roll(sp, 64, 1))
    srecv[col] = ssend[...]

    for d in HOPS:
        to = col_at(d)
        remote(ssend, srecv.at[col], 1, cols=to).start()
    for t in range(T):
        unpack(dat_r, t, (zmsg[0, t], zmsg[1, t], zmsg[2, t], zmsg[3, t], rowtile[t]))

    pick_j = lax.broadcasted_iota(jnp.int32, (64, 128), 0)
    pick_up = pick_j - jnp.where(lax.broadcasted_iota(jnp.int32, (64, 128), 1) < 64, 0, 8)

    def fill_pick(p, _):
        for which in range(4):
            base = 16 * which
            for i, (source, start) in enumerate(((pick_j, base), (pick_j, base + 8), (pick_up, base))):
                pick[p, :, pl.ds((which * 3 + i) * 128, 128)] = jnp.where(
                    source == start + p, 1.0, 0.0).astype(jnp.bfloat16)
        return 0

    lax.fori_loop(0, PAIRS, fill_pick, 0)

    for k in range(4):
        early, late = rate_ref[k, :8] * -LOG2E, rate_ref[k, 8:] * -LOG2E
        rt_ref[k, 0] = early[:, :128]
        rt_ref[k, 1] = late[:, :128]
        rt_ref[k, 2] = jnp.concatenate([early[:, 128:], late[:, 128:]], axis=1)

    def rates(k, p):
        return [jnp.broadcast_to(rt_ref[k, i, pl.ds(p, 1), :], (8, 128)) for i in range(3)]

    def load(dat, q, t):
        lo = dat[2 * q, t]
        return [lo, lo, dat[2 * q + 1, t]]

    W_A, W_D, R_A, R_D = 0, 1, 2, 3
    zero3 = [jnp.zeros((8, 128), F32)] * 3

    def coefs(wide, slot, t, which):
        return [wide[slot, pl.ds(t * 8, 8), pl.ds((which * 3 + i) * 128, 128)] for i in range(3)]

    def held(t, slot):
        return [decays[slot, t, i] for i in range(3)], [decays[slot, t, 3 + i] for i in range(3)]

    def local_pass(p, slot, dslot, ka, kd, dat, wide, tile):
        wide[slot] = jnp.dot(tile[:, :64], pick[p], preferred_element_type=F32)
        ra, rd = rates(ka, p), rates(kd, p)

        def up(t, carry):
            fa, md = carry[:3], carry[3:]
            s = load(dat, 0, t)
            da = tri(lambda a, b: jnp.exp2(a * b), s, ra)
            dd = tri(lambda a, b: jnp.exp2(a * b), s, rd)
            for i in range(3):
                decays[dslot, t, i] = da[i]
                decays[dslot, t, 3 + i] = dd[i]
            drive = tri(mul, load(dat, 1, t), coefs(wide, slot, t, W_A))
            fa = tri(add, tri(mul, da, fa), drive)
            md = tri(mul, dd, tri(add, tri(mul, load(dat, 2, t), coefs(wide, slot, t, R_D)), md))
            return (*fa, *md)

        def down(i, carry):
            t = T - 1 - i
            ma, fd = carry[:3], carry[3:]
            da, dd = held(t, dslot)
            drive = tri(mul, load(dat, 1, t), coefs(wide, slot, t, W_D))
            fd = tri(add, tri(mul, dd, fd), drive)
            ma = tri(mul, da, tri(add, tri(mul, load(dat, 2, t), coefs(wide, slot, t, R_A)), ma))
            return (*ma, *fd)

        a = lax.fori_loop(0, T, up, (*zero3, *zero3), unroll=True)
        b = lax.fori_loop(0, T, down, (*zero3, *zero3), unroll=True)
        return a[:3], b[:3], b[3:], a[3:]

    def final_pass(p, slot, dslot, ka, kd, dat, wide, acc, zbuf, starts):
        ra, rd = rates(ka, p), rates(kd, p)
        fa0, ma0, fd0, md0 = starts

        def put(q, t, parts):
            zbuf[q, p, 0, t], zbuf[q, p, 1, t] = fold(parts, low)

        def up(t, carry):
            h, m = carry[:3], carry[3:]
            da, dd = held(t, dslot)
            sx, g = load(dat, 1, t), load(dat, 2, t)
            db = tri(mul, da, h)
            h = tri(add, db, tri(mul, sx, coefs(wide, slot, t, W_A)))
            adj = tri(add, tri(mul, g, coefs(wide, slot, t, R_D)), m)
            for i in range(3):
                keep[t, i] = db[i]
                keep[t, 3 + i] = adj[i]
            put(2, t, tri(mul, h, g))
            put(1, t, tri(mul, adj, sx))
            th = tri(mul, adj, coefs(wide, slot, t, W_D))
            keep[t, 6] = th[0] + th[1]
            keep[t, 7] = th[2]
            return (*h, *tri(mul, dd, adj))

        def down(i, carry):
            t = T - 1 - i
            m, h, acc_a, acc_d = carry[:3], carry[3:6], carry[6:9], carry[9:]
            da, dd = held(t, dslot)
            s, sx, g = load(dat, 0, t), load(dat, 1, t), load(dat, 2, t)
            db = tri(mul, dd, h)
            h = tri(add, db, tri(mul, sx, coefs(wide, slot, t, W_D)))
            adj = tri(add, tri(mul, g, coefs(wide, slot, t, R_A)), m)
            put(3, t, tri(mul, h, g))
            put(0, t, tri(mul, adj, sx))
            th = tri(mul, adj, coefs(wide, slot, t, W_A))
            acc[0, t] += keep[t, 6] + (th[0] + th[1])
            acc[1, t] += keep[t, 7] + th[2]
            mem_a = tri(mul, adj, [keep[t, i] for i in range(3)])
            mem_d = tri(mul, [keep[t, 3 + i] for i in range(3)], db)
            mr = tri(add, tri(mul, mem_a, ra), tri(mul, mem_d, rd))
            acc[2, t] += mr[0] + mr[1]
            acc[3, t] += mr[2]
            acc_a = tri(add, acc_a, tri(mul, mem_a, s))
            acc_d = tri(add, acc_d, tri(mul, mem_d, s))
            return (*tri(mul, da, adj), *h, *acc_a, *acc_d)

        lax.fori_loop(0, T, up, (*fa0, *md0), unroll=True)
        out = lax.fori_loop(0, T, down, (*ma0, *fd0, *zero3, *zero3), unroll=True)
        for k, sums in ((ka, out[6:9]), (kd, out[9:])):
            for i in range(3):
                asend[k * PAIRS + p, pl.ds(i, 1), :] = -jnp.sum(sums[i], axis=0, keepdims=True)

    def channel_sums(zbuf):
        total = None
        for q in range(4):
            whole = jnp.concatenate(
                [zbuf[q, p, j].reshape(128, 128) for p in range(PAIRS) for j in range(2)], axis=1)
            high = whole.astype(jnp.bfloat16)
            rest = (whole - high.astype(F32)).astype(jnp.bfloat16)
            part = jnp.dot(high, place[q], preferred_element_type=F32)
            part = part + jnp.dot(rest, place[q], preferred_element_type=F32)
            total = part if total is None else total + part
        return total.reshape(T, 8, 128)

    def settle(acc, t):
        th, m = acc[1, t], acc[3, t]
        return jnp.where(low, th, m) + pltpu.roll(jnp.where(low, m, th), 64, 1)

    tile_r = rowtile[...].reshape(128, 128).astype(jnp.bfloat16)
    ztile[...] = tile_r

    def row_local(p, _):
        fa, ma, fd, md = local_pass(p, p, p, 0, 1, dat_r, spread_r, ztile)
        for q, parts in enumerate((fa, ma, fd, md)):
            for i in range(3):
                csend[q * PAIRS + p, i] = parts[i]
        return 0

    lax.fori_loop(0, PAIRS, row_local, 0, unroll=2)

    for d in HOPS:
        to = col_at(d)
        remote(csend.at[to], crecv.at[col], 2, cols=to).start()
    crecv[col] = csend[col]

    place_k = lax.broadcasted_iota(jnp.int32, (128, 128), 0) // 64 * 8
    place_n = lax.broadcasted_iota(jnp.int32, (128, 128), 1)

    def fill_place(p, _):
        for q in range(4):
            for j, source in enumerate((place_n - place_k, place_n + place_k - 8)):
                place[q, pl.ds(pl.multiple_of(p * 256 + j * 128, 128), 128), :] = jnp.where(
                    source == 16 * q + p, 1.0, 0.0).astype(jnp.bfloat16)
        return 0

    lax.fori_loop(0, PAIRS, fill_place, 0)
    skip = jnp.zeros((1, 192), F32)
    for r in range(8):
        skip = skip + jnp.sum(g_ref[r].astype(F32) * x_ref[r].astype(F32), axis=0, keepdims=True)
    skip_lo = skip[:, :128]
    skip_hi = jnp.concatenate([skip[:, 128:], skip[:, 128:]], axis=1)
    asend[...] = jnp.zeros_like(asend)
    asend[0, 3:4, :] = skip_lo
    asend[1, 3:4, :] = skip_hi
    acc_r[...] = jnp.zeros_like(acc_r)
    acc_z[...] = jnp.zeros_like(acc_z)
    shift[...] = jnp.zeros_like(shift)

    taken(srecv.at[pl.ds(0, COLS - 1)], recv_sem, 1)
    taken(crecv.at[pl.ds(0, COLS - 1)], recv_sem, 2)
    kind = col // PAIRS
    pair = lax.rem(col, PAIRS)
    falls = jnp.where((kind == 1) | (kind == 2), 1, 0)
    own_rates = rates(kind // 2, pair)

    def chain(i, carry):
        b = i + falls * (COLS - 1 - 2 * i)
        for j in range(3):
            bsend[b, j] = carry[j]
        s_lo, s_hi = srecv[b, 0], srecv[b, 1]
        kept = tri(lambda a, r: jnp.exp2(a * r), [s_lo, s_lo, s_hi], own_rates)
        return tuple(kept[j] * carry[j] + crecv[b, j] for j in range(3))

    lax.fori_loop(0, COLS, chain, tuple(zero3), unroll=True)

    for d in HOPS:
        to = col_at(d)
        remote(bsend.at[to], brecv.at[col], 3, cols=to).start()
    brecv[col] = bsend[col]

    taken(zrecv.at[:, pl.ds(0, 112), :], recv_sem, 0)
    for t in range(T):
        at = pl.ds(t, 8, stride=16)
        tiles = [zrecv[q, at, :] for q in range(5)]
        unpack(dat_z, t, tiles)
        rowtile[t] = tiles[4]
    ztile[...] = rowtile[...].reshape(128, 128).astype(jnp.bfloat16)
    chunk = lax.rem(lax.broadcasted_iota(jnp.int32, (8, 128), 0), 4)
    from_chunk = {1: [chunk >= d for d in (1, 2, 3)], -1: [chunk < 4 - d for d in (1, 2, 3)]}

    def shifted(j, d):
        return shift[j, pl.ds(16 - 2 * d, 8, stride=2), :]

    def set_shift(j, value):
        shift[j, pl.ds(16, 8, stride=2), :] = value

    zs = step_sums(dat_z)
    set_shift(12, zs[0])
    set_shift(13, zs[1])
    moved = tuple(shifted(j, d) for d in (1, 2, -1, -2) for j in (12, 13))

    def line_final(p, moved):
        ends = local_pass(p, 0, PAIRS, 2, 3, dat_z, spread_z, ztile)
        for e, parts in enumerate(ends):
            for i in range(3):
                set_shift(e * 3 + i, parts[i])
        starts = []
        for e, (k, sign) in enumerate(((2, 1), (2, -1), (3, -1), (3, 1))):
            rate = rates(k, p)
            at = 0 if sign == 1 else 4
            near, far = (moved[at], moved[at], moved[at + 1]), (moved[at + 2], moved[at + 2], moved[at + 3])
            start = []
            for i in range(3):
                f1, f2, f3 = (jnp.where(from_chunk[sign][d - 1], shifted(e * 3 + i, d * sign), 0.0)
                              for d in (1, 2, 3))
                start.append(f1 + jnp.exp2(near[i] * rate[i]) * (f2 + jnp.exp2(far[i] * rate[i]) * f3))
            starts.append(start)
        final_pass(p, 0, PAIRS, 2, 3, dat_z, spread_z, acc_z, zbuf_z, starts)
        return moved

    lax.fori_loop(0, PAIRS, line_final, moved, unroll=2)
    def send_a(first):
        def one(i, _):
            to = first + lax.rem(col + i, COLS // 2)

            @pl.when(to != col)
            def _():
                remote(asend.at[to], arecv.at[col], 5, cols=to).start()
            return 0

        lax.fori_loop(0, COLS // 2, one, 0)

    send_a(COLS // 2)

    taken(brecv.at[pl.ds(0, COLS - 1)], recv_sem, 3)

    def row_final(p, _):
        starts = [[brecv[q * PAIRS + p, i] for i in range(3)] for q in range(4)]
        final_pass(p, p, p, 0, 1, dat_r, spread_r, acc_r, zbuf_r, starts)
        return 0

    lax.fori_loop(0, PAIRS, row_final, 0, unroll=2)

    send_a(0)
    arecv[col] = asend[col]

    sums = channel_sums(zbuf_z)
    for t in range(T):
        at = pl.ds(t, 8, stride=16)
        zout[0, at, :] = acc_z[0, t]
        zout[1, at, :] = acc_z[2, t]
        zout[2, at, :] = settle(acc_z, t)
        zout[3, at, :] = sums[t]

    for d in ROW_HOPS:
        to = lax.rem(row + d, ROWS)
        for c in range(2):
            remote(zout.at[:, pl.ds(pl.multiple_of(c * 64 + to * 8, 8), 8), :],
                   zback.at[:, pl.ds(pl.multiple_of(row * 16 + c * 8, 8), 8), :], 4, rows=to).start()
    for c in range(2):
        zback[:, pl.ds(pl.multiple_of(row * 16 + c * 8, 8), 8), :] = (
            zout[:, pl.ds(pl.multiple_of(c * 64 + row * 8, 8), 8), :])

    taken(arecv.at[pl.ds(0, COLS - 1)], recv_sem, 5)
    zsum[row] = tree([arecv[b] for b in range(COLS)])

    for d in ROW_HOPS:
        to = lax.rem(row + d, ROWS)
        remote(zsum.at[row], zsum.at[row], 6, rows=to).start()

    sums = channel_sums(zbuf_r)
    for t in range(T):
        at = pl.ds(t, 8, stride=16)
        nat[0, at, :] = acc_r[0, t]
        nat[1, at, :] = acc_r[2, t]
        nat[2, at, :] = settle(acc_r, t)
        nat[3, at, :] = sums[t]

    taken(zsum.at[pl.ds(0, ROWS - 1)], recv_sem, 6)
    fin_ref[col] = tree([zsum[b] for b in range(ROWS)])

    for d in HOPS:
        to = col_at(d)
        remote(fin_ref.at[col], fin_ref.at[col], 7, cols=to).start()

    taken(zback.at[:, pl.ds(0, 112), :], recv_sem, 4)
    for r in range(8):
        back = pl.ds(r, 16, stride=8)
        at = pl.ds(r * 16, 16)
        th_lo = nat[0, at, :] + zback[0, back, :]
        m_lo = nat[1, at, :] + zback[1, back, :]
        packed = nat[2, at, :] + zback[2, back, :]
        th_hi = packed[:, :64]
        m_hi = pltpu.roll(packed, 64, 1)[:, :64]
        xv = x_ref[r].astype(F32)
        sv = s_ref[r].astype(F32)
        gv = g_ref[r].astype(F32)
        gi_ref[r, :, :128] = sk_ref[:, :128] * gv[:, :128] + sv[:, :128] * th_lo
        gi_ref[r, :, 128:] = sk_ref[:, 128:] * gv[:, 128:] + sv[:, 128:] * th_hi
        gs_ref[r, :, :128] = th_lo * xv[:, :128] + LN2 * m_lo
        gs_ref[r, :, 128:] = th_hi * xv[:, 128:] + LN2 * m_hi
        for first, sums in ((0, nat[3, at, :]), (2, zback[3, back, :])):
            for j in range(2):
                gw_ref[first + j, r] = sums[:, 16 * j : 16 * j + 16]
                gr_ref[first + j, r] = sums[:, 32 + 16 * j : 48 + 16 * j]

    leaving = [pltpu.make_async_copy(src, dst, out_sem.at[i]) for i, (src, dst) in enumerate(
        ((gi_ref, gi_out), (gs_ref, gs_out), (gw_ref, gw_out), (gr_ref, gr_out)))]
    for copy in leaving:
        copy.start()

    taken(fin_ref.at[pl.ds(0, COLS - 1)], recv_sem, 7)
    for k in range(4):
        lo, late, hi = (jnp.concatenate([fin_ref[k * PAIRS + p, pl.ds(i, 1), :] for p in range(PAIRS)], axis=0)
                        for i in range(3))
        rate_sum[k, :8, :128] = lo
        rate_sum[k, 8:, :128] = late
        rate_sum[k, :8, 128:] = hi[:, :64]
        rate_sum[k, 8:, 128:] = hi[:, 64:]
    skip_sum[:, :128] = fin_ref[0, 3:4, :]
    skip_sum[:, 128:] = fin_ref[1, 3:4, :64]
    last = [pltpu.make_async_copy(rate_sum, rate_out, out_sem.at[4]),
            pltpu.make_async_copy(skip_sum, skip_out, out_sem.at[5])]
    for copy in last:
        copy.start()

    taken(zrecv.at[:, pl.ds(0, 112), :], send_sem, 0)
    taken(srecv.at[pl.ds(0, COLS - 1)], send_sem, 1)
    taken(crecv.at[pl.ds(0, COLS - 1)], send_sem, 2)
    taken(brecv.at[pl.ds(0, COLS - 1)], send_sem, 3)
    taken(zback.at[:, pl.ds(0, 112), :], send_sem, 4)
    taken(arecv.at[pl.ds(0, COLS - 1)], send_sem, 5)
    taken(zsum.at[pl.ds(0, ROWS - 1)], send_sem, 6)
    taken(fin_ref.at[pl.ds(0, COLS - 1)], send_sem, 7)
    for copy in leaving + last:
        copy.wait()


def leave(*refs):
    ins, outs, held, sems = refs[:6], refs[6:12], refs[12:18], refs[18]
    arrive = [pltpu.make_async_copy(ins[i], held[i], sems.at[i]) for i in range(6)]
    depart = [pltpu.make_async_copy(held[i], outs[i], sems.at[6 + i]) for i in range(6)]
    for copy in arrive:
        copy.start()
    for i in range(6):
        arrive[i].wait()
        depart[i].start()
    for copy in depart:
        copy.wait()


def on_device(inputs, step_sizes, write_coef, read_coef, rate_table, skip_gain, grad_out):
    B16 = jnp.bfloat16
    scratch = [
        pltpu.VMEM(shape, kind[0] if kind else F32)
        for shape, *kind in (
            ((8, 16, 192),),
            ((8, 16, 192),),
            ((4, 8, 16, 16),),
            ((4, 8, 16, 16),),
            ((4, 16, 192),),
            ((1, 192),),
            ((COLS, 4, 128),),
            ((8, 16, 192), B16),
            ((8, 16, 192), B16),
            ((8, 16, 192), B16),
            ((4, 8, 16, 16), B16),
            ((4, 8, 16, 16), B16),
            ((4, 16, 192),),
            ((1, 192),),
            ((4, 3, PAIRS, 128),),
            ((6, 128, 128),),
            ((5, T, 8, 128),),
            ((T, 8, 128),),
            ((6, T, 8, 128),),
            ((6, T, 8, 128),),
            ((PAIRS + 1, T, 6, 8, 128),),
            ((2, 8, 128),),
            ((COLS, 2, 8, 128),),
            ((COLS, 3, 8, 128),),
            ((COLS, 3, 8, 128),),
            ((COLS, 3, 8, 128),),
            ((COLS, 3, 8, 128),),
            ((5, 128, 128),),
            ((128, 128), B16),
            ((T, 8, 8, 128),),
            ((4, T, 8, 128),),
            ((4, T, 8, 128),),
            ((4, PAIRS, 2, T, 8, 128),),
            ((4, PAIRS, 2, T, 8, 128),),
            ((PAIRS, 64, 12 * 128), B16),
            ((4, PAIRS * 256, 128), B16),
            ((PAIRS, 128, 12 * 128),),
            ((1, 128, 12 * 128),),
            ((14, 40, 128),),
            ((4, 128, 128),),
            ((4, 128, 128),),
            ((4, 128, 128),),
            ((COLS, 4, 128),),
            ((COLS, 4, 128),),
            ((ROWS, 4, 128),),
        )
    ]
    scratch += [pltpu.SemaphoreType.DMA((8,)), pltpu.SemaphoreType.DMA((8,)), pltpu.SemaphoreType.DMA((7,)), pltpu.SemaphoreType.DMA((6,))]
    cells = jax.ShapeDtypeStruct((8, 16, 192), F32)
    kinds = jax.ShapeDtypeStruct((4, 8, 16, 16), F32)
    shapes = [cells, cells, kinds, kinds, jax.ShapeDtypeStruct((4, 16, 192), F32), jax.ShapeDtypeStruct((1, 192), F32)]
    hbm = pl.BlockSpec(memory_space=pltpu.MemorySpace.HBM)
    made = pl.pallas_call(
        body,
        out_shape=shapes,
        in_specs=[hbm] * 7,
        out_specs=[hbm] * 6,
        scratch_shapes=scratch,
        compiler_params=pltpu.CompilerParams(
            collective_id=0, has_side_effects=True, vmem_limit_bytes=60 * 1024 * 1024),
    )(inputs, step_sizes, grad_out, write_coef, read_coef, rate_table.transpose(0, 2, 1), skip_gain.reshape(1, 192))
    gi, gs, gw, gr, rate, skip = pl.pallas_call(
        leave,
        out_shape=shapes,
        in_specs=[hbm] * 6,
        out_specs=[hbm] * 6,
        scratch_shapes=[pltpu.VMEM(a.shape, F32) for a in shapes] + [pltpu.SemaphoreType.DMA((12,))],
        compiler_params=pltpu.CompilerParams(vmem_limit_bytes=60 * 1024 * 1024),
    )(*made)
    return gi, gs, gw, gr, rate.transpose(0, 2, 1), skip.reshape(192)


def solution(mesh):
    cells, coefs = P("rows", "cols", None), P(None, "rows", "cols", None)
    return jax.shard_map(
        on_device, mesh=mesh, in_specs=(cells, cells, coefs, coefs, P(), P(), cells),
        out_specs=(cells, cells, coefs, coefs, P(), P()), check_vma=False)
```
